1024 devices in a mesh: replica: 16 (over y, core), mp: 64 (over z, x).
Axes of the slice: x: 4, y: 8, z: 16, core: 2. Of those that a mesh axis runs over, the one named last changes fastest.
Arguments:
- pooled: bfloat16 [262144, 4, 256], P(('replica', 'mp')), may hold values from -6 to 6
- row_ids: int32 [262144, 4, 2], P(('replica', 'mp')), may hold values from 0 to 131071, as said below
- labels: int32 [262144], P(('replica', 'mp')), may hold values 0 or 1
- row_slot: int32 [131072], replicated, may hold values from 0 to 131071, as said below
- w_hidden: bfloat16 [1024, 1024], replicated, may hold values from -0.1875 to 0.1875
- b_hidden: float32 [1024], replicated, may hold values from -4 to 4
- w_out: float32 [1024], replicated, may hold values from -0.1875 to 0.1875
- emb_table: float32 [131072, 256], P('mp'), may hold values from -4 to 4
- adam_moment: float32 [131072, 256], P(('mp', 'replica')), may hold values from -6 to 6
- adam_second: float32 [131072], P(('mp', 'replica')), may hold values from 0.5 to 4
Outputs:
- new_table: float32 [131072, 256], P('mp')
- new_moment: float32 [131072, 256], P(('mp', 'replica'))
- new_second: float32 [131072], P(('mp', 'replica'))
The draws below stay inside these ranges and needn't reach their ends.
Inputs may be any that keep to these rules, and one draw needn't show every extreme that they name: `row_slot`: a permutation of the table rows' storage positions; storage position p lies on index p // 2048 of mp, and its states on index (p % 2048) // 128 of replica. `row_ids`: the 2048 entries of each device's samples map, through row_slot, to every pair of an mp index and a replica index exactly 2 times; row ids repeat.
All inputs are finite; a program needn't handle non-finite values. No bound on the sum of `labels` on one device may be relied on, other than what follows from the above.
Results may differ from the reference program's by a relative error of at most 0.0032.
Values may be sent and summed in bfloat16 or wider, within the bound.
No kernel may reach another device: no remote copies, remote signals or barrier semaphores. Data moves between devices by JAX's collectives and lax.ppermute only.
A program may use at most 32 MiB of HBM per device.

```python
import math
import jax
import jax.numpy as jnp
from jax import lax

D = 256
H = 1024
F = 4
L = 2
SAMPLES = 256
ROWS_DEV = 2048
SHARD_ROWS = 128
ROWS = 131072
TOTAL = 262144
QUOTA = 2
DEVICES = 1024


def storage_layout(key):
    return jax.random.permutation(jax.random.fold_in(key, 11), ROWS).astype(jnp.int32)


def draw_row_slot(key, part):
    return storage_layout(key)


def draw_row_ids(key, part):
    layout = storage_layout(key)
    row_at = jnp.argsort(layout).astype(jnp.int32)
    key = jax.random.fold_in(key, 2)
    key_cells, key_upper, key_local = jax.random.split(key, 3)
    entries = SAMPLES * F * L
    reps = ROWS_DEV // SHARD_ROWS

    def shuffle_one(sub_key):
        return jax.random.permutation(sub_key, entries)
    shuffled = jax.vmap(shuffle_one)(jax.random.split(key_cells, DEVICES)).astype(jnp.int32)
    cell_idx = shuffled // QUOTA
    upper_lim = jax.random.randint(key_upper, (DEVICES, entries), 1, SHARD_ROWS + 1)
    local_row = jax.random.randint(key_local, (DEVICES, entries), 0, upper_lim)
    position = cell_idx // reps * ROWS_DEV + cell_idx % reps * SHARD_ROWS + local_row
    return row_at[position].reshape(TOTAL, F, L)


def set_ends(values, rng, smallest, top_value):
    place = [jax.random.randint(jax.random.fold_in(rng, axis), (), 0, length) for axis, length in enumerate(values.shape)]
    main_axis = values.shape.index(max(values.shape))
    next_to = place[:main_axis] + [(place[main_axis] + 1) % values.shape[main_axis]] + place[main_axis + 1:]
    return values.at[tuple(place)].set(smallest).at[tuple(next_to)].set(top_value)


def block_levels(stream_key, extent, cuts, low, largest):
    def one(dim, parts):
        steps = jax.random.uniform(jax.random.fold_in(jax.random.fold_in(stream_key, 6), dim), (parts,), jnp.float32, low / len(cuts), largest / len(cuts))
        return jnp.repeat(jnp.exp(steps), extent[dim] // parts).reshape((-1,) + (1,) * (len(extent) - dim - 1))

    loudness = one(*cuts[0])
    for cut in cuts[1:]:
        loudness = loudness * one(*cut)
    return loudness


def noise(stream_key, shape, spread, most, cuts=(), kind=jnp.bfloat16):
    factor_of = block_levels(stream_key, shape, cuts, -0.22, 0.18) if cuts else 1.0
    values = jax.random.normal(stream_key, shape, jnp.float32) * spread * factor_of
    return jnp.minimum(jnp.maximum(values, -most), most).astype(kind)


def setup_inputs(seed: int = 0) -> dict:
    seeds = jax.random.split(jax.random.key(seed), 11)
    return {
        "pooled": noise(seeds[0], (TOTAL, F, D), 1.0, 6.0, ((0, 1024),)),
        "row_ids": draw_row_ids(jax.random.fold_in(seeds[10], 71), 0),
        "labels": set_ends((jax.random.randint(seeds[2], (TOTAL,), 0, 3) < 1).astype(jnp.int32), jax.random.fold_in(seeds[2], 1), 0, 1),
        "row_slot": draw_row_slot(jax.random.fold_in(seeds[10], 71), 0),
        "w_hidden": noise(seeds[4], (F * D, H), (F * D) ** -0.5, 0.1875),
        "b_hidden": noise(seeds[5], (H,), 1.0, 4.0, (), jnp.float32),
        "w_out": noise(seeds[6], (H,), H ** -0.5, 0.1875, (), jnp.float32),
        "emb_table": noise(seeds[7], (ROWS, D), 0.5, 4.0, ((0, 64),), jnp.float32),
        "adam_moment": noise(seeds[8], (ROWS, D), 1.0, 6.0, ((0, 1024),), jnp.float32),
        "adam_second": jnp.clip(jnp.exp(math.log(4.0) - 2.0794415 * jax.random.uniform(seeds[9], (ROWS,), jnp.float32) ** block_levels(seeds[9], (ROWS,), ((0, 1024),), -0.2, 0.2)), 0.5, 4.0),
    }


LOSS_SCALE = 128.0
LEARN_RATE = 0.3
BETA_ONE = 0.8
BETA_TWO = 0.99
EPSILON = 1e-08

def pooled_grads(pooled, labels, w_hidden, b_hidden, w_out):
    batch_rows, num_feats, feat_width = pooled.shape
    features_flat = pooled.reshape(batch_rows, num_feats * feat_width)
    pre_act = jnp.dot(features_flat, w_hidden, preferred_element_type=jnp.float32) + b_hidden
    sig_pre = jax.nn.sigmoid(pre_act)
    hidden = pre_act * sig_pre
    logit = lax.optimization_barrier(jnp.sum(hidden * w_out[None, :], axis=1))
    probability = jax.nn.sigmoid(logit)
    target = labels.astype(jnp.float32)
    dlogit = -LOSS_SCALE * (1.0 - probability * probability) * (target - (1.0 - target) * probability)
    dpre = (dlogit[:, None] * w_out[None, :] * (sig_pre * (1.0 + pre_act * (1.0 - sig_pre)))).astype(jnp.bfloat16)
    dflat = lax.dot_general(dpre, w_hidden, (((1,), (1,)), ((), ())), preferred_element_type=jnp.float32)
    return dflat.astype(jnp.bfloat16).reshape(batch_rows, num_feats, feat_width)

def reference(pooled, row_ids, labels, row_slot, w_hidden, b_hidden, w_out, emb_table, adam_moment, adam_second):

    def one_group(pieces):
        return pooled_grads(pieces[0], pieces[1], w_hidden, b_hidden, w_out)
    grads = lax.map(one_group, (pooled.reshape(DEVICES, SAMPLES, F, D), labels.reshape(DEVICES, SAMPLES)))
    grads_wide = grads.reshape(TOTAL * F, D).astype(jnp.float32)
    positions = row_slot[row_ids]
    grad_total = jnp.zeros((ROWS, D), jnp.float32)
    for slot_idx in range(L):
        grad_total = grad_total + jax.ops.segment_sum(grads_wide, positions[:, :, slot_idx].reshape(-1), num_segments=ROWS)
    new_moment = BETA_ONE * adam_moment + (1.0 - BETA_ONE) * grad_total
    new_second = BETA_TWO * adam_second + (1.0 - BETA_TWO) * lax.optimization_barrier(jnp.mean(grad_total * grad_total, axis=1))
    new_table = emb_table - LEARN_RATE * new_moment / (jnp.sqrt(new_second)[:, None] + EPSILON)
    return (new_table, new_moment, new_second)
```

```python
import jax
import jax.numpy as jnp
from jax import lax
from jax.experimental import pallas as pl
from jax.experimental.pallas import tpu as pltpu
from jax.sharding import PartitionSpec as P

LOSS_SCALE = 128.0
LEARN_RATE = 0.3
BETA_ONE = 0.8
BETA_TWO = 0.99
EPSILON = 1e-08

BF = jnp.bfloat16
F32 = jnp.float32
I32 = jnp.int32
LIMIT = 40 * 1024 * 1024


def iota(shape, dim):
    return lax.broadcasted_iota(I32, shape, dim)


def dot(a, b):
    return jnp.dot(a, b, preferred_element_type=F32)


def dot_t(a, b):
    return lax.dot_general(a, b, (((1,), (1,)), ((), ())), preferred_element_type=F32)


def onehot(cond):
    return jnp.where(cond, 1.0, 0.0).astype(BF)


def call(body, outs, *args, scratch=(), smem=0, alias=None):
    specs = [pl.BlockSpec(memory_space=pltpu.SMEM)] * smem
    specs += [pl.BlockSpec(memory_space=pltpu.VMEM)] * (len(args) - smem)
    return pl.pallas_call(
        body,
        out_shape=outs,
        in_specs=specs,
        out_specs=[pl.BlockSpec(memory_space=pltpu.VMEM)] * len(outs),
        scratch_shapes=list(scratch),
        compiler_params=pltpu.CompilerParams(vmem_limit_bytes=LIMIT),
    )(*args)


def route_body(ids_ref, map_ref, slot_ref, local_ref, pieces, owners, cells):
    feats, bag, batch = ids_ref.shape
    hi_count, lo_count = map_ref.shape
    mapped = map_ref[...].astype(F32).T.astype(I32)
    pieces[0:lo_count, :] = (mapped & 127).astype(F32).astype(BF)
    pieces[lo_count : 2 * lo_count, :] = ((mapped >> 7) & 15).astype(F32).astype(BF)
    pieces[2 * lo_count :, :] = (mapped >> 11).astype(F32).astype(BF)
    count = feats * bag
    sums = jnp.zeros((64, 32), F32)
    locs, ys, cs, ms = [], [], [], []
    lane = iota((1, batch), 1).astype(F32)
    for fl in range(count):
        ids = ids_ref[fl // bag, fl % bag : fl % bag + 1, :]
        hit = onehot(iota((hi_count, batch), 0) == (ids >> 7))
        found = dot(pieces[...], hit)
        mask = iota((lo_count, batch), 0) == (ids & 127)

        def pick(k):
            part = found[k * lo_count : (k + 1) * lo_count, :]
            return jnp.sum(jnp.where(mask, part, 0.0), axis=0, keepdims=True)

        loc, rep, own = pick(0), pick(1).astype(I32), pick(2).astype(I32)
        y, c = rep >> 1, rep & 1
        owner = onehot(iota((64, batch), 0) == own)
        cell = jnp.where(iota((16, batch), 0) == c * 8 + y, 1.0, 0.0)
        owners[fl] = owner
        cells[fl] = cell
        terms = jnp.concatenate([cell * float(fl), cell * lane], axis=0).astype(BF)
        sums += dot_t(owner, terms)
        locs.append(loc)
        ys.append(y)
        cs.append(c)
        ms.append(own)
    total = sums[:, :16] * float(batch) + sums[:, 16:]
    top = jnp.floor(total * (1.0 / 64.0))
    halves = jnp.concatenate([top, total - 64.0 * top], axis=1).T.astype(BF)
    local = jnp.zeros((64, 32), F32)
    for fl in range(count):
        seen = dot(halves, owners[fl])
        pair = jnp.sum(cells[fl] * (64.0 * seen[:16] + seen[16:]), axis=0, keepdims=True)
        rank = (pair < 2.0 * (lane + float(fl * batch))).astype(I32)
        lead = cs[fl] * 2 + rank
        slot_ref[fl : fl + 1, :] = (ys[fl] * 64 + ms[fl]) * 4 + lead
        spread = jnp.where(iota((32, batch), 0) == lead * 8 + ys[fl], locs[fl], 0.0)
        local += dot_t(owners[fl], spread.astype(BF))
    local_ref[...] = local


def pack_body(slot_ref, grads_ref, send_ref):
    batch, wide = grads_ref.shape
    width = 256
    step = 512
    for chunk in range(2048 // step):
        rows = iota((step, batch), 0) + chunk * step
        acc = jnp.zeros((step, width), F32)
        for f in range(wide // width):
            a = slot_ref[2 * f : 2 * f + 1, :]
            b = slot_ref[2 * f + 1 : 2 * f + 2, :]
            take = onehot((rows == a) | (rows == b))
            acc += dot(take, grads_ref[:, f * width : (f + 1) * width])
        left = acc[:, :128].reshape(step // 8, 8, 128)
        right = acc[:, 128:].reshape(step // 8, 8, 128)
        low = iota((step // 8, 8, 128), 1) < 4
        first = jnp.where(low, left, pltpu.roll(right, 4, axis=1))
        second = jnp.where(low, pltpu.roll(left, 4, axis=1), right)
        both = jnp.concatenate([first[:, None], second[:, None]], axis=1)
        send_ref[chunk * 2 * step : (chunk + 1) * 2 * step, :] = both.reshape(2 * step, 128).astype(BF)


def total_body(core_ref, local_ref, got_ref, own_ref, sib_ref):
    core = core_ref[0]
    n = iota((256, 512), 1)
    order = onehot(iota((256, 512), 0) == (n & 3) * 64 + (n >> 3))
    spot = dot(local_ref[...].astype(BF), order).astype(I32)
    n = iota((8, 512), 1)
    spot = spot + ((n >> 2) & 1) * 256 + (((n >> 1) & 1) ^ core) * 128
    acc = jnp.zeros((512, 128), F32)
    for y in range(8):
        hit = onehot(iota((512, 512), 0) == spot[y : y + 1, :])
        acc += dot(hit, got_ref[y * 512 : (y + 1) * 512, :])
    own_ref[:, :128] = acc[0:128]
    own_ref[:, 128:] = acc[256:384]
    sib_ref[:, :128] = acc[128:256]
    sib_ref[:, 128:] = acc[384:512]


def adam_body(own_ref, sib_ref, moment_ref, second_ref, new_moment_ref, new_second_ref, step_ref):
    grad = own_ref[...] + sib_ref[...]
    moment = BETA_ONE * moment_ref[...] + (1.0 - BETA_ONE) * grad
    mean = jnp.sum(grad * grad, axis=1, keepdims=True) * (1.0 / grad.shape[1])
    rows = grad.shape[0]
    eye = iota((rows, rows), 0) == iota((rows, rows), 1)
    old = jnp.sum(jnp.where(eye, second_ref[...], 0.0), axis=1, keepdims=True)
    second = BETA_TWO * old + (1.0 - BETA_TWO) * mean
    new_moment_ref[...] = moment
    new_second_ref[...] = jnp.sum(jnp.where(eye, second, 0.0), axis=0, keepdims=True)
    step_ref[...] = (LEARN_RATE * moment / (jnp.sqrt(second) + EPSILON)).astype(BF)


def pooled_grads(pooled, labels, w_hidden, b_hidden, w_out):
    batch_rows, num_feats, feat_width = pooled.shape
    features_flat = pooled.reshape(batch_rows, num_feats * feat_width)
    pre_act = jnp.dot(features_flat, w_hidden, preferred_element_type=F32) + b_hidden
    sig_pre = jax.nn.sigmoid(pre_act)
    hidden = pre_act * sig_pre
    logit = jnp.sum(hidden * w_out[None, :], axis=1)
    probability = jax.nn.sigmoid(logit)
    target = labels.astype(F32)
    dlogit = (
        -LOSS_SCALE * (1.0 - probability * probability) * (target - (1.0 - target) * probability)
    )
    dpre = (
        dlogit[:, None] * w_out[None, :] * (sig_pre * (1.0 + pre_act * (1.0 - sig_pre)))
    ).astype(BF)
    dflat = lax.dot_general(
        dpre, w_hidden, (((1,), (1,)), ((), ())), preferred_element_type=F32
    )
    return dflat.astype(BF)


def on_device(
    pooled,
    row_ids,
    labels,
    row_slot,
    w_hidden,
    b_hidden,
    w_out,
    emb_table,
    adam_moment,
    adam_second,
):
    shape = jax.ShapeDtypeStruct
    rep, mp = "replica", "mp"
    same_core = [[2 * y + c for y in range(8)] for c in range(2)]
    planes = [[r * 64 + m for r in group for m in range(64)] for group in same_core]
    other_core = [(i, i ^ 1) for i in range(16)]
    core = lax.axis_index(rep) % 2

    slots, local = call(
        route_body,
        [shape((8, 256), I32), shape((64, 32), F32)],
        row_ids.transpose(1, 2, 0),
        row_slot.reshape(1024, 128),
        scratch=[
            pltpu.VMEM((384, 1024), BF),
            pltpu.VMEM((8, 64, 256), BF),
            pltpu.VMEM((8, 16, 256), F32),
        ],
    )
    local = lax.all_to_all(
        local.reshape(64, 1, 32), mp, split_axis=0, concat_axis=0, tiled=True
    )
    grads = pooled_grads(pooled, labels, w_hidden, b_hidden, w_out)
    (send,) = call(pack_body, [shape((4096, 128), BF)], slots, grads)
    got = lax.all_to_all(
        send.reshape(512, 8, 128),
        (rep, mp),
        split_axis=0,
        concat_axis=0,
        tiled=True,
        axis_index_groups=planes,
    )
    local = local.reshape(64, 4, 8).transpose(2, 1, 0).reshape(8, 1, 256)
    local = lax.all_to_all(
        local, rep, split_axis=0, concat_axis=0, tiled=True, axis_index_groups=same_core
    )
    own, sib = call(
        total_body,
        [shape((128, 256), F32), shape((128, 256), F32)],
        core.reshape(1).astype(I32),
        local.reshape(8, 256),
        got.reshape(4096, 128),
        smem=1,
    )
    sib = lax.ppermute(sib, rep, other_core)
    new_moment, new_second, step = call(
        adam_body,
        [shape((128, 256), F32), shape((1, 128), F32), shape((128, 256), BF)],
        own,
        sib,
        adam_moment,
        adam_second.reshape(1, 128),
    )
    mine = lax.all_gather(step, rep, axis=0, tiled=False, axis_index_groups=same_core)
    others = lax.ppermute(mine, rep, other_core)
    even = jnp.where(core == 0, mine, others)
    odd = jnp.where(core == 0, others, mine)
    steps = jnp.stack([even, odd], axis=1).reshape(2048, 256)
    new_table = emb_table - steps.astype(F32)
    return (new_table, new_moment, new_second.reshape(128))


def solution(mesh):
    in_specs = (
        P(("replica", "mp"), None, None),
        P(("replica", "mp"), None, None),
        P(("replica", "mp")),
        P(),
        P(),
        P(),
        P(),
        P("mp", None),
        P(("mp", "replica"), None),
        P(("mp", "replica")),
    )
    out_specs = (P("mp", None), P(("mp", "replica"), None), P(("mp", "replica")))
    return jax.shard_map(
        on_device, mesh=mesh, in_specs=in_specs, out_specs=out_specs, check_vma=False
    )
```

```python
import jax
import jax.numpy as jnp
from jax import lax
from jax.experimental import pallas as pl
from jax.experimental.pallas import tpu as pltpu
from jax.sharding import PartitionSpec as P

LOSS_SCALE = 128.0
LEARN_RATE = 0.3
BETA_ONE = 0.8
BETA_TWO = 0.99
EPSILON = 1e-08

BF = jnp.bfloat16
F32 = jnp.float32
I32 = jnp.int32
LIMIT = 40 * 1024 * 1024


def iota(shape, dim):
    return lax.broadcasted_iota(I32, shape, dim)


def dot(a, b):
    return jnp.dot(a, b, preferred_element_type=F32)


def dot_t(a, b):
    return lax.dot_general(a, b, (((1,), (1,)), ((), ())), preferred_element_type=F32)


def onehot(cond):
    return jnp.where(cond, 1.0, 0.0).astype(BF)


def call(body, outs, *args, scratch=(), smem=0, alias=None):
    specs = [pl.BlockSpec(memory_space=pltpu.SMEM)] * smem
    specs += [pl.BlockSpec(memory_space=pltpu.VMEM)] * (len(args) - smem)
    return pl.pallas_call(
        body,
        out_shape=outs,
        in_specs=specs,
        out_specs=[pl.BlockSpec(memory_space=pltpu.VMEM)] * len(outs),
        scratch_shapes=list(scratch),
        compiler_params=pltpu.CompilerParams(vmem_limit_bytes=LIMIT),
    )(*args)


def route_body(ids_ref, map_ref, slot_ref, local_ref, pieces, owners, cells):
    feats, bag, batch = ids_ref.shape
    hi_count, lo_count = map_ref.shape
    mapped = map_ref[...].astype(F32).T.astype(I32)
    pieces[0:lo_count, :] = (mapped & 127).astype(F32).astype(BF)
    pieces[lo_count : 2 * lo_count, :] = ((mapped >> 7) & 15).astype(F32).astype(BF)
    pieces[2 * lo_count :, :] = (mapped >> 11).astype(F32).astype(BF)
    count = feats * bag
    sums = jnp.zeros((64, 32), F32)
    locs, ys, cs, ms = [], [], [], []
    lane = iota((1, batch), 1).astype(F32)
    for fl in range(count):
        ids = ids_ref[fl // bag, fl % bag : fl % bag + 1, :]
        hit = onehot(iota((hi_count, batch), 0) == (ids >> 7))
        found = dot(pieces[...], hit)
        mask = iota((lo_count, batch), 0) == (ids & 127)

        def pick(k):
            part = found[k * lo_count : (k + 1) * lo_count, :]
            return jnp.sum(jnp.where(mask, part, 0.0), axis=0, keepdims=True)

        loc, rep, own = pick(0), pick(1).astype(I32), pick(2).astype(I32)
        y, c = rep >> 1, rep & 1
        owner = onehot(iota((64, batch), 0) == own)
        cell = jnp.where(iota((16, batch), 0) == c * 8 + y, 1.0, 0.0)
        owners[fl] = owner
        cells[fl] = cell
        terms = jnp.concatenate([cell * float(fl), cell * lane], axis=0).astype(BF)
        sums += dot_t(owner, terms)
        locs.append(loc)
        ys.append(y)
        cs.append(c)
        ms.append(own)
    total = sums[:, :16] * float(batch) + sums[:, 16:]
    top = jnp.floor(total * (1.0 / 64.0))
    halves = jnp.concatenate([top, total - 64.0 * top], axis=1).T.astype(BF)
    local = jnp.zeros((64, 32), F32)
    for fl in range(count):
        seen = dot(halves, owners[fl])
        pair = jnp.sum(cells[fl] * (64.0 * seen[:16] + seen[16:]), axis=0, keepdims=True)
        rank = (pair < 2.0 * (lane + float(fl * batch))).astype(I32)
        lead = cs[fl] * 2 + rank
        slot_ref[fl : fl + 1, :] = (ys[fl] * 64 + ms[fl]) * 4 + lead
        spread = jnp.where(iota((32, batch), 0) == lead * 8 + ys[fl], locs[fl], 0.0)
        local += dot_t(owners[fl], spread.astype(BF))
    turned = local.T
    local_ref[...] = jnp.concatenate([turned[:16], turned[16:]], axis=1).astype(BF)


def pack_body(slot_ref, grads_ref, send_ref):
    batch, wide = grads_ref.shape
    width = 256
    step = 512
    for chunk in range(2048 // step):
        rows = iota((step, batch), 0) + chunk * step
        acc = jnp.zeros((step, width), F32)
        for f in range(wide // width):
            a = slot_ref[2 * f : 2 * f + 1, :]
            b = slot_ref[2 * f + 1 : 2 * f + 2, :]
            take = onehot((rows == a) | (rows == b))
            acc += dot(take, grads_ref[:, f * width : (f + 1) * width])
        left = acc[:, :128].reshape(step // 8, 8, 128)
        right = acc[:, 128:].reshape(step // 8, 8, 128)
        low = iota((step // 8, 8, 128), 1) < 4
        first = jnp.where(low, left, pltpu.roll(right, 4, axis=1))
        second = jnp.where(low, pltpu.roll(left, 4, axis=1), right)
        both = jnp.concatenate([first[:, None], second[:, None]], axis=1)
        send_ref[chunk * 2 * step : (chunk + 1) * 2 * step, :] = both.reshape(2 * step, 128).astype(BF)


def select_body(place_ref, all_ref, mine_ref):
    rows, lanes = iota((8, 128), 0), iota((8, 128), 1)
    take = onehot(lanes == rows * 64 + place_ref[0])
    mine_ref[...] = dot_t(take, all_ref[...])[:2]


def total_body(place_ref, local_ref, got_ref, own_ref, sib_ref):
    y_here, core = place_ref[1], place_ref[2]
    n = iota((1024, 512), 1)
    order = onehot(iota((1024, 512), 0) == (n >> 3) * 16 + (n & 1) * 8 + y_here)
    found = dot(local_ref[...].astype(BF), order).reshape(8, 2, 512)
    n = iota((8, 512), 1)
    side = (n >> 1) & 1
    spot = jnp.where(side == 0, found[:, 0, :], found[:, 1, :]).astype(I32)
    spot = spot + ((n >> 2) & 1) * 256 + (side ^ core) * 128
    acc = jnp.zeros((512, 128), F32)
    for y in range(8):
        hit = onehot(iota((512, 512), 0) == spot[y : y + 1, :])
        acc += dot(hit, got_ref[y * 512 : (y + 1) * 512, :])
    own_ref[:, :128] = acc[0:128]
    own_ref[:, 128:] = acc[256:384]
    sib_ref[:, :128] = acc[128:256]
    sib_ref[:, 128:] = acc[384:512]


def adam_body(own_ref, sib_ref, moment_ref, second_ref, new_moment_ref, new_second_ref, step_ref):
    grad = own_ref[...] + sib_ref[...]
    moment = BETA_ONE * moment_ref[...] + (1.0 - BETA_ONE) * grad
    mean = jnp.sum(grad * grad, axis=1, keepdims=True) * (1.0 / grad.shape[1])
    rows = grad.shape[0]
    eye = iota((rows, rows), 0) == iota((rows, rows), 1)
    old = jnp.sum(jnp.where(eye, second_ref[...], 0.0), axis=1, keepdims=True)
    second = BETA_TWO * old + (1.0 - BETA_TWO) * mean
    new_moment_ref[...] = moment
    new_second_ref[...] = jnp.sum(jnp.where(eye, second, 0.0), axis=0, keepdims=True)
    step_ref[...] = (LEARN_RATE * moment / (jnp.sqrt(second) + EPSILON)).astype(BF)


def table_body(place_ref, mine_ref, others_ref, table_ref, out_ref):
    core = place_ref[2]
    for steps, side in ((mine_ref, core), (others_ref, 1 - core)):
        rows = pl.ds(pl.multiple_of(side * 128, 128), 128)
        out_ref[rows, :] = table_ref[rows, :] - steps[0].astype(F32)


def pooled_grads(pooled, labels, w_hidden, b_hidden, w_out):
    batch_rows, num_feats, feat_width = pooled.shape
    features_flat = pooled.reshape(batch_rows, num_feats * feat_width)
    pre_act = jnp.dot(features_flat, w_hidden, preferred_element_type=F32) + b_hidden
    sig_pre = jax.nn.sigmoid(pre_act)
    hidden = pre_act * sig_pre
    logit = jnp.sum(hidden * w_out[None, :], axis=1)
    probability = jax.nn.sigmoid(logit)
    target = labels.astype(F32)
    dlogit = (
        -LOSS_SCALE * (1.0 - probability * probability) * (target - (1.0 - target) * probability)
    )
    dpre = (
        dlogit[:, None] * w_out[None, :] * (sig_pre * (1.0 + pre_act * (1.0 - sig_pre)))
    ).astype(BF)
    dflat = lax.dot_general(
        dpre, w_hidden, (((1,), (1,)), ((), ())), preferred_element_type=F32
    )
    return dflat.astype(BF)


def on_device(
    pooled,
    row_ids,
    labels,
    row_slot,
    w_hidden,
    b_hidden,
    w_out,
    emb_table,
    adam_moment,
    adam_second,
):
    shape = jax.ShapeDtypeStruct
    rep, mp = "replica", "mp"
    same_core = [[2 * y + c for y in range(8)] for c in range(2)]
    planes = [[r * 64 + m for r in group for m in range(64)] for group in same_core]
    other_core = [(i, i ^ 1) for i in range(16)]
    core = lax.axis_index(rep) & 1
    place = jnp.stack([lax.axis_index(mp), lax.axis_index(rep) >> 1, core]).astype(I32)

    slots, local = call(
        route_body,
        [shape((8, 256), I32), shape((16, 128), BF)],
        row_ids.transpose(1, 2, 0),
        row_slot.reshape(1024, 128),
        scratch=[
            pltpu.VMEM((384, 1024), BF),
            pltpu.VMEM((8, 64, 256), BF),
            pltpu.VMEM((8, 16, 256), F32),
        ],
    )
    grads = pooled_grads(pooled, labels, w_hidden, b_hidden, w_out)
    (send,) = call(pack_body, [shape((4096, 128), BF)], slots, grads)
    send, local = lax.optimization_barrier((send, local))
    got = lax.all_to_all(
        send.reshape(512, 8, 128),
        (rep, mp),
        split_axis=0,
        concat_axis=0,
        tiled=True,
        axis_index_groups=planes,
    )
    local = lax.all_gather(local, mp, axis=0, tiled=True)
    (local,) = call(select_body, [shape((2, 1024), F32)], place, local, smem=1)
    local = lax.all_gather(local, rep, axis=0, tiled=True, axis_index_groups=same_core)
    own, sib = call(
        total_body,
        [shape((128, 256), F32), shape((128, 256), F32)],
        place,
        local,
        got.reshape(4096, 128),
        smem=1,
    )
    sib = lax.ppermute(sib, rep, other_core)
    new_moment, new_second, step = call(
        adam_body,
        [shape((128, 256), F32), shape((1, 128), F32), shape((128, 256), BF)],
        own,
        sib,
        adam_moment,
        adam_second.reshape(1, 128),
    )
    mine = lax.all_gather(step, rep, axis=0, tiled=False, axis_index_groups=same_core)
    others = lax.ppermute(mine, rep, other_core)
    new_table = pl.pallas_call(
        table_body,
        grid=(8,),
        out_shape=shape((2048, 256), F32),
        in_specs=[
            pl.BlockSpec(memory_space=pltpu.SMEM),
            pl.BlockSpec((1, 128, 256), lambda i: (i, 0, 0)),
            pl.BlockSpec((1, 128, 256), lambda i: (i, 0, 0)),
            pl.BlockSpec((256, 256), lambda i: (i, 0)),
        ],
        out_specs=pl.BlockSpec((256, 256), lambda i: (i, 0)),
    )(place, mine, others, emb_table)
    return (new_table, new_moment, new_second.reshape(128))


def solution(mesh):
    in_specs = (
        P(("replica", "mp"), None, None),
        P(("replica", "mp"), None, None),
        P(("replica", "mp")),
        P(),
        P(),
        P(),
        P(),
        P("mp", None),
        P(("mp", "replica"), None),
        P(("mp", "replica")),
    )
    out_specs = (P("mp", None), P(("mp", "replica"), None), P(("mp", "replica")))
    return jax.shard_map(
        on_device, mesh=mesh, in_specs=in_specs, out_specs=out_specs, check_vma=False
    )
```

```python
import jax
import jax.numpy as jnp
from jax import lax
from jax.experimental import pallas as pl
from jax.experimental.pallas import tpu as pltpu
from jax.sharding import PartitionSpec as P

LOSS_SCALE = 128.0
LEARN_RATE = 0.3
BETA_ONE = 0.8
BETA_TWO = 0.99
EPSILON = 1e-08

BF = jnp.bfloat16
F32 = jnp.float32
I32 = jnp.int32
LIMIT = 40 * 1024 * 1024


def iota(shape, dim):
    return lax.broadcasted_iota(I32, shape, dim)


def dot(a, b):
    return jnp.dot(a, b, preferred_element_type=F32)


def dot_t(a, b):
    return lax.dot_general(a, b, (((1,), (1,)), ((), ())), preferred_element_type=F32)


def onehot(cond):
    return jnp.where(cond, 1.0, 0.0).astype(BF)


def call(body, outs, *args, scratch=(), smem=0, alias=None):
    specs = [pl.BlockSpec(memory_space=pltpu.SMEM)] * smem
    specs += [pl.BlockSpec(memory_space=pltpu.VMEM)] * (len(args) - smem)
    return pl.pallas_call(
        body,
        out_shape=outs,
        in_specs=specs,
        out_specs=[pl.BlockSpec(memory_space=pltpu.VMEM)] * len(outs),
        scratch_shapes=list(scratch),
        compiler_params=pltpu.CompilerParams(vmem_limit_bytes=LIMIT),
    )(*args)


def route_body(ids_ref, map_ref, slot_ref, local_ref, pieces, owners, cells):
    feats, bag, batch = ids_ref.shape
    hi_count, lo_count = map_ref.shape
    mapped = map_ref[...].astype(F32).T.astype(I32)
    pieces[0:lo_count, :] = (mapped & 127).astype(F32).astype(BF)
    pieces[lo_count : 2 * lo_count, :] = ((mapped >> 7) & 15).astype(F32).astype(BF)
    pieces[2 * lo_count :, :] = (mapped >> 11).astype(F32).astype(BF)
    count = feats * bag
    sums = jnp.zeros((64, 32), F32)
    locs, ys, cs, ms = [], [], [], []
    lane = iota((1, batch), 1).astype(F32)
    for fl in range(count):
        ids = ids_ref[fl // bag, fl % bag : fl % bag + 1, :]
        hit = onehot(iota((hi_count, batch), 0) == (ids >> 7))
        found = dot(pieces[...], hit)
        mask = iota((lo_count, batch), 0) == (ids & 127)

        def pick(k):
            part = found[k * lo_count : (k + 1) * lo_count, :]
            return jnp.sum(jnp.where(mask, part, 0.0), axis=0, keepdims=True)

        loc, rep, own = pick(0), pick(1).astype(I32), pick(2).astype(I32)
        y, c = rep >> 1, rep & 1
        owner = onehot(iota((64, batch), 0) == own)
        cell = jnp.where(iota((16, batch), 0) == c * 8 + y, 1.0, 0.0)
        owners[fl] = owner
        cells[fl] = cell
        terms = jnp.concatenate([cell * float(fl), cell * lane], axis=0).astype(BF)
        sums += dot_t(owner, terms)
        locs.append(loc)
        ys.append(y)
        cs.append(c)
        ms.append(own)
    total = sums[:, :16] * float(batch) + sums[:, 16:]
    top = jnp.floor(total * (1.0 / 64.0))
    halves = jnp.concatenate([top, total - 64.0 * top], axis=1).T.astype(BF)
    local = jnp.zeros((64, 32), F32)
    for fl in range(count):
        seen = dot(halves, owners[fl])
        pair = jnp.sum(cells[fl] * (64.0 * seen[:16] + seen[16:]), axis=0, keepdims=True)
        rank = (pair < 2.0 * (lane + float(fl * batch))).astype(I32)
        lead = cs[fl] * 2 + rank
        slot_ref[fl : fl + 1, :] = (ys[fl] * 64 + ms[fl]) * 4 + lead
        spread = jnp.where(iota((32, batch), 0) == lead * 8 + ys[fl], locs[fl], 0.0)
        local += dot_t(owners[fl], spread.astype(BF))
    local_ref[...] = local


def pack_body(slot_ref, grads_ref, send_ref):
    batch, wide = grads_ref.shape
    width = 256
    step = 512
    for chunk in range(2048 // step):
        rows = iota((step, batch), 0) + chunk * step
        acc = jnp.zeros((step, width), F32)
        for f in range(wide // width):
            a = slot_ref[2 * f : 2 * f + 1, :]
            b = slot_ref[2 * f + 1 : 2 * f + 2, :]
            take = onehot((rows == a) | (rows == b))
            acc += dot(take, grads_ref[:, f * width : (f + 1) * width])
        left = acc[:, :128].reshape(step // 8, 8, 128)
        right = acc[:, 128:].reshape(step // 8, 8, 128)
        low = iota((step // 8, 8, 128), 1) < 4
        first = jnp.where(low, left, pltpu.roll(right, 4, axis=1))
        second = jnp.where(low, pltpu.roll(left, 4, axis=1), right)
        both = jnp.concatenate([first[:, None], second[:, None]], axis=1)
        send_ref[chunk * 2 * step : (chunk + 1) * 2 * step, :] = both.reshape(2 * step, 128).astype(BF)


def total_body(place_ref, local_ref, got_ref, own_ref, sib_ref):
    y_here, core = place_ref[0], place_ref[1]
    n = iota((32, 512), 1)
    pick = onehot(iota((32, 512), 0) == (n & 3) * 8 + y_here)
    near = iota((64, 512), 0) == iota((64, 512), 1) >> 3
    n = iota((1, 512), 1)
    shift = ((n >> 2) & 1) * 256 + (((n >> 1) & 1) ^ core) * 128
    acc = jnp.zeros((512, 128), F32)
    for y in range(8):
        found = dot(local_ref[y].astype(BF), pick)
        spot = jnp.sum(jnp.where(near, found, 0.0), axis=0, keepdims=True).astype(I32) + shift
        hit = onehot(iota((512, 512), 0) == spot)
        acc += dot(hit, got_ref[y * 512 : (y + 1) * 512, :])
    own_ref[:, :128] = acc[0:128]
    own_ref[:, 128:] = acc[256:384]
    sib_ref[:, :128] = acc[128:256]
    sib_ref[:, 128:] = acc[384:512]


def adam_body(own_ref, sib_ref, moment_ref, second_ref, new_moment_ref, new_second_ref, step_ref):
    grad = own_ref[...] + sib_ref[...]
    moment = BETA_ONE * moment_ref[...] + (1.0 - BETA_ONE) * grad
    mean = jnp.sum(grad * grad, axis=1, keepdims=True) * (1.0 / grad.shape[1])
    rows = grad.shape[0]
    eye = iota((rows, rows), 0) == iota((rows, rows), 1)
    old = jnp.sum(jnp.where(eye, second_ref[...], 0.0), axis=1, keepdims=True)
    second = BETA_TWO * old + (1.0 - BETA_TWO) * mean
    new_moment_ref[...] = moment
    new_second_ref[...] = jnp.sum(jnp.where(eye, second, 0.0), axis=0, keepdims=True)
    step_ref[...] = (LEARN_RATE * moment / (jnp.sqrt(second) + EPSILON)).astype(BF)


def pooled_grads(pooled, labels, w_hidden, b_hidden, w_out):
    batch_rows, num_feats, feat_width = pooled.shape
    features_flat = pooled.reshape(batch_rows, num_feats * feat_width)
    pre_act = jnp.dot(features_flat, w_hidden, preferred_element_type=F32) + b_hidden
    sig_pre = jax.nn.sigmoid(pre_act)
    hidden = pre_act * sig_pre
    logit = jnp.sum(hidden * w_out[None, :], axis=1)
    probability = jax.nn.sigmoid(logit)
    target = labels.astype(F32)
    dlogit = (
        -LOSS_SCALE * (1.0 - probability * probability) * (target - (1.0 - target) * probability)
    )
    dpre = (
        dlogit[:, None] * w_out[None, :] * (sig_pre * (1.0 + pre_act * (1.0 - sig_pre)))
    ).astype(BF)
    dflat = lax.dot_general(
        dpre, w_hidden, (((1,), (1,)), ((), ())), preferred_element_type=F32
    )
    return dflat.astype(BF)


def on_device(
    pooled,
    row_ids,
    labels,
    row_slot,
    w_hidden,
    b_hidden,
    w_out,
    emb_table,
    adam_moment,
    adam_second,
):
    shape = jax.ShapeDtypeStruct
    rep, mp = "replica", "mp"
    same_core = [[2 * y + c for y in range(8)] for c in range(2)]
    planes = [[r * 64 + m for r in group for m in range(64)] for group in same_core]
    other_core = [(i, i ^ 1) for i in range(16)]
    core = lax.axis_index(rep) & 1
    place = jnp.stack([lax.axis_index(rep) >> 1, core]).astype(I32)

    slots, local = call(
        route_body,
        [shape((8, 256), I32), shape((64, 32), F32)],
        row_ids.transpose(1, 2, 0),
        row_slot.reshape(1024, 128),
        scratch=[
            pltpu.VMEM((384, 1024), BF),
            pltpu.VMEM((8, 64, 256), BF),
            pltpu.VMEM((8, 16, 256), F32),
        ],
    )
    local = lax.all_to_all(
        local.reshape(64, 1, 32), mp, split_axis=0, concat_axis=0, tiled=True
    )
    grads = pooled_grads(pooled, labels, w_hidden, b_hidden, w_out)
    (send,) = call(pack_body, [shape((4096, 128), BF)], slots, grads)
    send, local = lax.optimization_barrier((send, local))
    got = lax.all_to_all(
        send.reshape(512, 8, 128),
        (rep, mp),
        split_axis=0,
        concat_axis=0,
        tiled=True,
        axis_index_groups=planes,
    )
    local = lax.all_gather(
        local.reshape(64, 32), rep, axis=0, tiled=False, axis_index_groups=same_core
    )
    own, sib = call(
        total_body,
        [shape((128, 256), F32), shape((128, 256), F32)],
        place,
        local,
        got.reshape(4096, 128),
        smem=1,
    )
    sib = lax.ppermute(sib, rep, other_core)
    new_moment, new_second, step = call(
        adam_body,
        [shape((128, 256), F32), shape((1, 128), F32), shape((128, 256), BF)],
        own,
        sib,
        adam_moment,
        adam_second.reshape(1, 128),
    )
    mine = lax.all_gather(step, rep, axis=0, tiled=False, axis_index_groups=same_core)
    others = lax.ppermute(mine, rep, other_core)
    even = jnp.where(core == 0, mine, others)
    odd = jnp.where(core == 0, others, mine)
    steps = jnp.stack([even, odd], axis=1).reshape(2048, 256)
    new_table = emb_table - steps.astype(F32)
    return (new_table, new_moment, new_second.reshape(128))


def solution(mesh):
    in_specs = (
        P(("replica", "mp"), None, None),
        P(("replica", "mp"), None, None),
        P(("replica", "mp")),
        P(),
        P(),
        P(),
        P(),
        P("mp", None),
        P(("mp", "replica"), None),
        P(("mp", "replica")),
    )
    out_specs = (P("mp", None), P(("mp", "replica"), None), P(("mp", "replica")))
    return jax.shard_map(
        on_device, mesh=mesh, in_specs=in_specs, out_specs=out_specs, check_vma=False
    )
```

```python
import jax
import jax.numpy as jnp
from jax import lax
from jax.experimental import pallas as pl
from jax.experimental.pallas import tpu as pltpu
from jax.sharding import PartitionSpec as P

LOSS_SCALE = 128.0
LEARN_RATE = 0.3
BETA_ONE = 0.8
BETA_TWO = 0.99
EPSILON = 1e-08

BF = jnp.bfloat16
F32 = jnp.float32
I32 = jnp.int32
LIMIT = 32 * 1024 * 1024
HEAD = 112


def iota(shape, dim):
    return lax.broadcasted_iota(I32, shape, dim)


def dot(a, b):
    return jnp.dot(a, b, preferred_element_type=F32)


def dot_t(a, b):
    return lax.dot_general(a, b, (((1,), (1,)), ((), ())), preferred_element_type=F32)


def onehot(cond):
    return jnp.where(cond, 1.0, 0.0).astype(BF)


def call(body, outs, *args, scratch=(), smem=0, alias=None):
    specs = [pl.BlockSpec(memory_space=pltpu.SMEM)] * smem
    specs += [pl.BlockSpec(memory_space=pltpu.VMEM)] * (len(args) - smem)
    return pl.pallas_call(
        body,
        out_shape=outs,
        in_specs=specs,
        out_specs=[pl.BlockSpec(memory_space=pltpu.VMEM)] * len(outs),
        scratch_shapes=list(scratch),
        compiler_params=pltpu.CompilerParams(vmem_limit_bytes=LIMIT),
    )(*args)


def route_body(ids_ref, map_ref, slot_ref, local_ref, pieces, owners, cells):
    feats, bag, batch = ids_ref.shape
    hi_count, lo_count = map_ref.shape
    mapped = map_ref[...].astype(F32).T
    high = jnp.floor(mapped * (1.0 / 256.0))
    pieces[0:lo_count, :] = (mapped - 256.0 * high).astype(BF)
    pieces[lo_count:, :] = (high - 256.0).astype(BF)
    count = feats * bag
    sums = jnp.zeros((64, 32), F32)
    locs, ys, cs, ms = [], [], [], []
    lane = iota((1, batch), 1).astype(F32)
    for fl in range(count):
        ids = ids_ref[fl // bag, fl % bag : fl % bag + 1, :]
        hit = onehot(iota((hi_count, batch), 0) == (ids >> 7))
        found = dot(pieces[...], hit)
        mask = iota((lo_count, batch), 0) == (ids & 127)

        def pick(k):
            part = found[k * lo_count : (k + 1) * lo_count, :]
            return jnp.sum(jnp.where(mask, part, 0.0), axis=0, keepdims=True)

        low, high = pick(0).astype(I32), pick(1).astype(I32) + 256
        loc = (low & 127).astype(F32)
        own, y, c = high >> 3, high & 7, low >> 7
        owner = onehot(iota((64, batch), 0) == own)
        cell = jnp.where(iota((16, batch), 0) == c * 8 + y, 1.0, 0.0)
        owners[fl] = owner
        cells[fl] = cell
        terms = jnp.concatenate([cell * float(fl), cell * lane], axis=0).astype(BF)
        sums += dot_t(owner, terms)
        locs.append(loc)
        ys.append(y)
        cs.append(c)
        ms.append(own)
    total = sums[:, :16] * float(batch) + sums[:, 16:]
    top = jnp.floor(total * (1.0 / 64.0))
    halves = jnp.concatenate([top, total - 64.0 * top], axis=1).T.astype(BF)
    local = jnp.zeros((64, 32), F32)
    for fl in range(count):
        seen = dot(halves, owners[fl])
        pair = jnp.sum(cells[fl] * (64.0 * seen[:16] + seen[16:]), axis=0, keepdims=True)
        rank = (pair < 2.0 * (lane + float(fl * batch))).astype(I32)
        lead = cs[fl] * 2 + rank
        slot_ref[fl : fl + 1, :] = (ys[fl] * 64 + ms[fl]) * 4 + lead
        spread = jnp.where(iota((32, batch), 0) == lead * 8 + ys[fl], locs[fl], 0.0)
        local += dot_t(owners[fl], spread.astype(BF))
    local_ref[...] = local


def pack_body(slot_ref, grads_ref, send_ref):
    batch, wide = grads_ref.shape
    width = 256
    step = 512
    for chunk in range(2048 // step):
        rows = iota((step, batch), 0) + chunk * step
        acc = jnp.zeros((step, width), F32)
        for f in range(wide // width):
            a = slot_ref[2 * f : 2 * f + 1, :]
            b = slot_ref[2 * f + 1 : 2 * f + 2, :]
            take = onehot((rows == a) | (rows == b))
            acc += dot(take, grads_ref[:, f * width : (f + 1) * width])
        left = acc[:, :128].reshape(step // 8, 8, 128)
        right = acc[:, 128:].reshape(step // 8, 8, 128)
        low = iota((step // 8, 8, 128), 1) < 4
        first = jnp.where(low, left, pltpu.roll(right, 4, axis=1))
        second = jnp.where(low, pltpu.roll(left, 4, axis=1), right)
        both = jnp.concatenate([first[:, None], second[:, None]], axis=1)
        send_ref[chunk * 2 * step : (chunk + 1) * 2 * step, :] = both.reshape(2 * step, 128).astype(BF)


def spots_body(place_ref, local_ref, spots_ref):
    y_here, core = place_ref[0], place_ref[1]
    n = iota((32, 512), 1)
    pick = onehot(iota((32, 512), 0) == (n & 3) * 8 + y_here)
    near = iota((64, 512), 0) == iota((64, 512), 1) >> 3
    n = iota((1, 512), 1)
    shift = ((n >> 2) & 1) * 256 + (((n >> 1) & 1) ^ core) * 128
    for y in range(8):
        found = dot(local_ref[y].astype(BF), pick)
        spot = jnp.sum(jnp.where(near, found, 0.0), axis=0, keepdims=True).astype(I32)
        spots_ref[y : y + 1, :] = spot + shift


def total_body(spots_ref, got_ref, own_ref, sib_ref):
    acc = jnp.zeros((512, 128), F32)
    for y in range(8):
        hit = onehot(iota((512, 512), 0) == spots_ref[y : y + 1, :])
        acc += dot(hit, got_ref[y * 512 : (y + 1) * 512, :])
    own_ref[:, :128] = acc[0:128]
    own_ref[:, 128:] = acc[256:384]
    sib_ref[:, :128] = acc[128:256]
    sib_ref[:, 128:] = acc[384:512]


def adam_body(own_ref, sib_ref, moment_ref, second_ref, new_moment_ref, new_second_ref, head_ref, tail_ref):
    grad = own_ref[...] + sib_ref[...]
    moment = BETA_ONE * moment_ref[...] + (1.0 - BETA_ONE) * grad
    mean = jnp.sum(grad * grad, axis=1, keepdims=True) * (1.0 / grad.shape[1])
    rows = grad.shape[0]
    eye = iota((rows, rows), 0) == iota((rows, rows), 1)
    old = jnp.sum(jnp.where(eye, second_ref[...], 0.0), axis=1, keepdims=True)
    second = BETA_TWO * old + (1.0 - BETA_TWO) * mean
    new_moment_ref[...] = moment
    new_second_ref[...] = jnp.sum(jnp.where(eye, second, 0.0), axis=0, keepdims=True)
    step = (LEARN_RATE * moment / (jnp.sqrt(second) + EPSILON)).astype(BF)
    head_ref[...] = step[:HEAD]
    tail_ref[...] = jnp.broadcast_to(step[HEAD:][None], tail_ref.shape)


def table_body(head_ref, tail_ref, table_ref, out_ref, rows_ref, in_sems, out_sems):
    parts = in_sems.shape[0]
    size = rows_ref.shape[0] // parts

    def span(i):
        return pl.ds(i * size, size)

    loads = [
        pltpu.make_async_copy(table_ref.at[span(i)], rows_ref.at[span(i)], in_sems.at[i])
        for i in range(parts)
    ]
    stores = [
        pltpu.make_async_copy(rows_ref.at[span(i)], out_ref.at[span(i)], out_sems.at[i])
        for i in range(parts)
    ]
    for load in loads:
        load.start()
    for i in range(parts):
        loads[i].wait()
        for r in range(i * size // 128, (i + 1) * size // 128):
            mid = r * 128 + HEAD
            rows_ref[r * 128 : mid, :] -= head_ref[r].astype(F32)
            rows_ref[mid : (r + 1) * 128, :] -= tail_ref[r].astype(F32)
        stores[i].start()
    for store in stores:
        store.wait()


def pooled_grads(pooled, labels, w_hidden, b_hidden, w_out):
    batch_rows, num_feats, feat_width = pooled.shape
    features_flat = pooled.reshape(batch_rows, num_feats * feat_width)
    pre_act = jnp.dot(features_flat, w_hidden, preferred_element_type=F32) + b_hidden
    sig_pre = jax.nn.sigmoid(pre_act)
    hidden = pre_act * sig_pre
    logit = jnp.sum(hidden * w_out[None, :], axis=1)
    probability = jax.nn.sigmoid(logit)
    target = labels.astype(F32)
    dlogit = (
        -LOSS_SCALE * (1.0 - probability * probability) * (target - (1.0 - target) * probability)
    )
    dpre = (
        dlogit[:, None] * w_out[None, :] * (sig_pre * (1.0 + pre_act * (1.0 - sig_pre)))
    ).astype(BF)
    dflat = lax.dot_general(
        dpre, w_hidden, (((1,), (1,)), ((), ())), preferred_element_type=F32
    )
    return dflat.astype(BF)


def on_device(
    pooled,
    row_ids,
    labels,
    row_slot,
    w_hidden,
    b_hidden,
    w_out,
    emb_table,
    adam_moment,
    adam_second,
):
    shape = jax.ShapeDtypeStruct
    rep, mp = "replica", "mp"
    same_core = [[2 * y + c for y in range(8)] for c in range(2)]
    planes = [[r * 64 + m for r in group for m in range(64)] for group in same_core]
    other_core = [(i, i ^ 1) for i in range(16)]
    core = lax.axis_index(rep) & 1
    place = jnp.stack([lax.axis_index(rep) >> 1, core]).astype(I32)

    slots, local = call(
        route_body,
        [shape((8, 256), I32), shape((64, 32), F32)],
        row_ids.transpose(1, 2, 0),
        row_slot.reshape(1024, 128),
        scratch=[
            pltpu.VMEM((256, 1024), BF),
            pltpu.VMEM((8, 64, 256), BF),
            pltpu.VMEM((8, 16, 256), F32),
        ],
    )
    local = lax.all_to_all(
        local.reshape(64, 1, 32), mp, split_axis=0, concat_axis=0, tiled=True
    )
    grads = pooled_grads(pooled, labels, w_hidden, b_hidden, w_out)
    (send,) = call(pack_body, [shape((4096, 128), BF)], slots, grads)
    send, local = lax.optimization_barrier((send, local))
    got = lax.all_to_all(
        send.reshape(512, 8, 128),
        (rep, mp),
        split_axis=0,
        concat_axis=0,
        tiled=True,
        axis_index_groups=planes,
    )
    local = lax.all_gather(
        local.reshape(64, 32), rep, axis=0, tiled=False, axis_index_groups=same_core
    )
    (spots,) = call(spots_body, [shape((8, 512), I32)], place, local, smem=1)
    own, sib = call(
        total_body,
        [shape((128, 256), F32), shape((128, 256), F32)],
        spots,
        got.reshape(4096, 128),
    )
    sib = lax.ppermute(sib, rep, other_core)
    new_moment, new_second, head, tail = call(
        adam_body,
        [
            shape((128, 256), F32),
            shape((1, 128), F32),
            shape((HEAD, 256), BF),
            shape((16, 128 - HEAD, 256), BF),
        ],
        own,
        sib,
        adam_moment,
        adam_second.reshape(1, 128),
    )
    tails = lax.all_to_all(tail, rep, split_axis=0, concat_axis=0, tiled=True)
    heads = lax.all_gather(head, rep, axis=0, tiled=False)
    vmem, hbm = pl.BlockSpec(memory_space=pltpu.VMEM), pl.BlockSpec(memory_space=pltpu.HBM)
    new_table = pl.pallas_call(
        table_body,
        out_shape=shape((2048, 256), F32),
        in_specs=[vmem, vmem, hbm],
        out_specs=hbm,
        scratch_shapes=[
            pltpu.VMEM((2048, 256), F32),
            pltpu.SemaphoreType.DMA((4,)),
            pltpu.SemaphoreType.DMA((4,)),
        ],
        compiler_params=pltpu.CompilerParams(vmem_limit_bytes=51 * 1024 * 1024),
    )(heads, tails, emb_table)
    return (new_table, new_moment, new_second.reshape(128))


def solution(mesh):
    in_specs = (
        P(("replica", "mp"), None, None),
        P(("replica", "mp"), None, None),
        P(("replica", "mp")),
        P(),
        P(),
        P(),
        P(),
        P("mp", None),
        P(("mp", "replica"), None),
        P(("mp", "replica")),
    )
    out_specs = (P("mp", None), P(("mp", "replica"), None), P(("mp", "replica")))
    return jax.shard_map(
        on_device, mesh=mesh, in_specs=in_specs, out_specs=out_specs, check_vma=False
    )
```

```python
import jax
import jax.numpy as jnp
from jax import lax
from jax.experimental import pallas as pl
from jax.experimental.pallas import tpu as pltpu
from jax.sharding import PartitionSpec as P

LOSS_SCALE = 128.0
LEARN_RATE = 0.3
BETA_ONE = 0.8
BETA_TWO = 0.99
EPSILON = 1e-08

BF = jnp.bfloat16
F32 = jnp.float32
I32 = jnp.int32
LIMIT = 32 * 1024 * 1024
HEAD = 112


def iota(shape, dim):
    return lax.broadcasted_iota(I32, shape, dim)


def dot(a, b):
    return jnp.dot(a, b, preferred_element_type=F32)


def dot_t(a, b):
    return lax.dot_general(a, b, (((1,), (1,)), ((), ())), preferred_element_type=F32)


def onehot(cond):
    return jnp.where(cond, 1.0, 0.0).astype(BF)


def call(body, outs, *args, scratch=(), smem=0, alias=None):
    specs = [pl.BlockSpec(memory_space=pltpu.SMEM)] * smem
    specs += [pl.BlockSpec(memory_space=pltpu.VMEM)] * (len(args) - smem)
    return pl.pallas_call(
        body,
        out_shape=outs,
        in_specs=specs,
        out_specs=[pl.BlockSpec(memory_space=pltpu.VMEM)] * len(outs),
        scratch_shapes=list(scratch),
        compiler_params=pltpu.CompilerParams(vmem_limit_bytes=LIMIT),
    )(*args)


def route_body(ids_ref, map_ref, slot_ref, local_ref, pieces, owners, cells):
    feats, bag, batch = ids_ref.shape
    hi_count, lo_count = map_ref.shape
    mapped = map_ref[...].astype(F32).T
    high = jnp.floor(mapped * (1.0 / 256.0))
    pieces[0:lo_count, :] = (mapped - 256.0 * high).astype(BF)
    pieces[lo_count:, :] = (high - 256.0).astype(BF)
    count = feats * bag
    sums = jnp.zeros((64, 32), F32)
    locs, ys, cs, ms = [], [], [], []
    m_here, y_here = lax.axis_index("mp"), lax.axis_index("replica") >> 1
    lane = iota((1, batch), 1).astype(F32)
    for fl in range(count):
        ids = ids_ref[fl // bag, fl % bag : fl % bag + 1, :]
        hit = onehot(iota((hi_count, batch), 0) == (ids >> 7))
        found = dot(pieces[...], hit)
        mask = iota((lo_count, batch), 0) == (ids & 127)

        def pick(k):
            part = found[k * lo_count : (k + 1) * lo_count, :]
            return jnp.sum(jnp.where(mask, part, 0.0), axis=0, keepdims=True)

        low, high = pick(0).astype(I32), pick(1).astype(I32) + 256
        loc = (low & 127).astype(F32)
        own, y, c = high >> 3, high & 7, low >> 7
        owner = onehot(iota((64, batch), 0) == own ^ m_here)
        cell = jnp.where(iota((16, batch), 0) == c * 8 + (y ^ y_here), 1.0, 0.0)
        owners[fl] = owner
        cells[fl] = cell
        terms = jnp.concatenate([cell * float(fl), cell * lane], axis=0).astype(BF)
        sums += dot_t(owner, terms)
        locs.append(loc)
        ys.append(y)
        cs.append(c)
        ms.append(own)
    total = sums[:, :16] * float(batch) + sums[:, 16:]
    top = jnp.floor(total * (1.0 / 64.0))
    halves = jnp.concatenate([top, total - 64.0 * top], axis=1).T.astype(BF)
    local = jnp.zeros((64, 32), F32)
    for fl in range(count):
        seen = dot(halves, owners[fl])
        pair = jnp.sum(cells[fl] * (64.0 * seen[:16] + seen[16:]), axis=0, keepdims=True)
        rank = (pair < 2.0 * (lane + float(fl * batch))).astype(I32)
        lead = cs[fl] * 2 + rank
        slot_ref[fl : fl + 1, :] = (ys[fl] * 64 + ms[fl]) * 4 + lead
        spread = jnp.where(iota((32, batch), 0) == lead * 8 + (ys[fl] ^ y_here), locs[fl], 0.0)
        local += dot_t(owners[fl], spread.astype(BF))
    turned = local.T
    local_ref[...] = jnp.concatenate([turned[:16], turned[16:]], axis=1)


def pack_body(slot_ref, grads_ref, send_ref):
    batch, wide = grads_ref.shape
    width = 256
    step = 512
    for chunk in range(2048 // step):
        rows = iota((step, batch), 0) + chunk * step
        acc = jnp.zeros((step, width), F32)
        for f in range(wide // width):
            a = slot_ref[2 * f : 2 * f + 1, :]
            b = slot_ref[2 * f + 1 : 2 * f + 2, :]
            take = onehot((rows == a) | (rows == b))
            acc += dot(take, grads_ref[:, f * width : (f + 1) * width])
        left = acc[:, :128].reshape(step // 8, 8, 128)
        right = acc[:, 128:].reshape(step // 8, 8, 128)
        low = iota((step // 8, 8, 128), 1) < 4
        first = jnp.where(low, left, pltpu.roll(right, 4, axis=1))
        second = jnp.where(low, pltpu.roll(left, 4, axis=1), right)
        both = jnp.concatenate([first[:, None], second[:, None]], axis=1)
        send_ref[chunk * 2 * step : (chunk + 1) * 2 * step, :] = both.reshape(2 * step, 128).astype(BF)


def spots_body(local_ref, spots_ref):
    here = lax.axis_index("replica")
    y_here, core = here >> 1, here & 1
    n = iota((128, 512), 1)
    lane = ((n >> 1) & 1) * 64 + ((n >> 3) ^ lax.axis_index("mp"))
    found = dot(local_ref[...].astype(BF), onehot(iota((128, 512), 0) == lane)).astype(BF)
    row = iota((8, 16), 0) ^ y_here
    place = iota((8, 16), 1)
    first = dot(onehot(place == row), found)
    second = dot(onehot(place == row + 8), found)
    n = iota((8, 512), 1)
    spot = jnp.where((n & 1) == 0, first, second).astype(I32)
    spots_ref[...] = spot + ((n >> 2) & 1) * 256 + (((n >> 1) & 1) ^ core) * 128


def total_body(spots_ref, got_ref, own_ref, sib_ref):
    acc = jnp.zeros((512, 128), F32)
    for y in range(8):
        hit = onehot(iota((512, 512), 0) == spots_ref[y : y + 1, :])
        acc += dot(hit, got_ref[y * 512 : (y + 1) * 512, :])
    own_ref[:, :128] = acc[0:128]
    own_ref[:, 128:] = acc[256:384]
    sib_ref[:, :128] = acc[128:256]
    sib_ref[:, 128:] = acc[384:512]


def adam_body(own_ref, sib_ref, moment_ref, second_ref, new_moment_ref, new_second_ref, head_ref, tail_ref):
    grad = own_ref[...] + sib_ref[...]
    moment = BETA_ONE * moment_ref[...] + (1.0 - BETA_ONE) * grad
    mean = jnp.sum(grad * grad, axis=1, keepdims=True) * (1.0 / grad.shape[1])
    rows = grad.shape[0]
    eye = iota((rows, rows), 0) == iota((rows, rows), 1)
    old = jnp.sum(jnp.where(eye, second_ref[...], 0.0), axis=1, keepdims=True)
    second = BETA_TWO * old + (1.0 - BETA_TWO) * mean
    new_moment_ref[...] = moment
    new_second_ref[...] = jnp.sum(jnp.where(eye, second, 0.0), axis=0, keepdims=True)
    step = (LEARN_RATE * moment / (jnp.sqrt(second) + EPSILON)).astype(BF)
    head_ref[...] = step[:HEAD]
    tail_ref[...] = jnp.broadcast_to(step[HEAD:][None], tail_ref.shape)


def table_body(head_ref, tail_ref, table_ref, out_ref, rows_ref, in_sems, out_sems):
    parts = in_sems.shape[0]
    size = rows_ref.shape[0] // parts

    def span(i):
        return pl.ds(i * size, size)

    loads = [
        pltpu.make_async_copy(table_ref.at[span(i)], rows_ref.at[span(i)], in_sems.at[i])
        for i in range(parts)
    ]
    stores = [
        pltpu.make_async_copy(rows_ref.at[span(i)], out_ref.at[span(i)], out_sems.at[i])
        for i in range(parts)
    ]
    for load in loads:
        load.start()
    for i in range(parts):
        loads[i].wait()
        for r in range(i * size // 128, (i + 1) * size // 128):
            mid = r * 128 + HEAD
            rows_ref[r * 128 : mid, :] -= head_ref[r].astype(F32)
            rows_ref[mid : (r + 1) * 128, :] -= tail_ref[r].astype(F32)
        stores[i].start()
    for store in stores:
        store.wait()


def pooled_grads(pooled, labels, w_hidden, b_hidden, w_out):
    batch_rows, num_feats, feat_width = pooled.shape
    features_flat = pooled.reshape(batch_rows, num_feats * feat_width)
    pre_act = jnp.dot(features_flat, w_hidden, preferred_element_type=F32) + b_hidden
    sig_pre = jax.nn.sigmoid(pre_act)
    hidden = pre_act * sig_pre
    logit = jnp.sum(hidden * w_out[None, :], axis=1)
    probability = jax.nn.sigmoid(logit)
    target = labels.astype(F32)
    dlogit = (
        -LOSS_SCALE * (1.0 - probability * probability) * (target - (1.0 - target) * probability)
    )
    dpre = (
        dlogit[:, None] * w_out[None, :] * (sig_pre * (1.0 + pre_act * (1.0 - sig_pre)))
    ).astype(BF)
    dflat = lax.dot_general(
        dpre, w_hidden, (((1,), (1,)), ((), ())), preferred_element_type=F32
    )
    return dflat.astype(BF)


def on_device(
    pooled,
    row_ids,
    labels,
    row_slot,
    w_hidden,
    b_hidden,
    w_out,
    emb_table,
    adam_moment,
    adam_second,
):
    shape = jax.ShapeDtypeStruct
    rep, mp = "replica", "mp"
    same_core = [[2 * y + c for y in range(8)] for c in range(2)]
    planes = [[r * 64 + m for r in group for m in range(64)] for group in same_core]
    other_core = [(i, i ^ 1) for i in range(16)]
    slots, local = call(
        route_body,
        [shape((8, 256), I32), shape((16, 128), F32)],
        row_ids.transpose(1, 2, 0),
        row_slot.reshape(1024, 128),
        scratch=[
            pltpu.VMEM((256, 1024), BF),
            pltpu.VMEM((8, 64, 256), BF),
            pltpu.VMEM((8, 16, 256), F32),
        ],
    )
    grads = pooled_grads(pooled, labels, w_hidden, b_hidden, w_out)
    (send,) = call(pack_body, [shape((4096, 128), BF)], slots, grads)
    send, local = lax.optimization_barrier((send, local))
    got = lax.all_to_all(
        send.reshape(512, 8, 128),
        (rep, mp),
        split_axis=0,
        concat_axis=0,
        tiled=True,
        axis_index_groups=planes,
    )
    rows, lanes = iota((16, 128), 0), iota((16, 128), 1)
    for bit in (1, 2, 4):
        other = lax.ppermute(local, rep, [(i, i ^ (2 * bit)) for i in range(16)])
        local = jnp.where((rows & bit) != 0, other, local)
    for bit in (1, 2, 4, 8, 16, 32):
        other = lax.ppermute(local, mp, [(i, i ^ bit) for i in range(64)])
        local = jnp.where((lanes & bit) != 0, other, local)
    (spots,) = call(spots_body, [shape((8, 512), I32)], local)
    own, sib = call(
        total_body,
        [shape((128, 256), F32), shape((128, 256), F32)],
        spots,
        got.reshape(4096, 128),
    )
    sib = lax.ppermute(sib, rep, other_core)
    new_moment, new_second, head, tail = call(
        adam_body,
        [
            shape((128, 256), F32),
            shape((1, 128), F32),
            shape((HEAD, 256), BF),
            shape((16, 128 - HEAD, 256), BF),
        ],
        own,
        sib,
        adam_moment,
        adam_second.reshape(1, 128),
    )
    tails = lax.all_to_all(tail, rep, split_axis=0, concat_axis=0, tiled=True)
    heads = lax.all_gather(head, rep, axis=0, tiled=False)
    vmem, hbm = pl.BlockSpec(memory_space=pltpu.VMEM), pl.BlockSpec(memory_space=pltpu.HBM)
    new_table = pl.pallas_call(
        table_body,
        out_shape=shape((2048, 256), F32),
        in_specs=[vmem, vmem, hbm],
        out_specs=hbm,
        scratch_shapes=[
            pltpu.VMEM((2048, 256), F32),
            pltpu.SemaphoreType.DMA((4,)),
            pltpu.SemaphoreType.DMA((4,)),
        ],
        compiler_params=pltpu.CompilerParams(vmem_limit_bytes=51 * 1024 * 1024),
    )(heads, tails, emb_table)
    return (new_table, new_moment, new_second.reshape(128))


def solution(mesh):
    in_specs = (
        P(("replica", "mp"), None, None),
        P(("replica", "mp"), None, None),
        P(("replica", "mp")),
        P(),
        P(),
        P(),
        P(),
        P("mp", None),
        P(("mp", "replica"), None),
        P(("mp", "replica")),
    )
    out_specs = (P("mp", None), P(("mp", "replica"), None), P(("mp", "replica")))
    return jax.shard_map(
        on_device, mesh=mesh, in_specs=in_specs, out_specs=out_specs, check_vma=False
    )
```

```python
import jax
import jax.numpy as jnp
from jax import lax
from jax.experimental import pallas as pl
from jax.experimental.pallas import tpu as pltpu
from jax.sharding import PartitionSpec as P

LOSS_SCALE = 128.0
LEARN_RATE = 0.3
BETA_ONE = 0.8
BETA_TWO = 0.99
EPSILON = 1e-08

BF = jnp.bfloat16
F32 = jnp.float32
I32 = jnp.int32
LIMIT = 32 * 1024 * 1024
HEAD = 112


def iota(shape, dim):
    return lax.broadcasted_iota(I32, shape, dim)


def dot(a, b):
    return jnp.dot(a, b, preferred_element_type=F32)


def dot_t(a, b):
    return lax.dot_general(a, b, (((1,), (1,)), ((), ())), preferred_element_type=F32)


def onehot(cond):
    return jnp.where(cond, 1.0, 0.0).astype(BF)


def call(body, outs, *args, scratch=(), smem=0, alias=None):
    specs = [pl.BlockSpec(memory_space=pltpu.SMEM)] * smem
    specs += [pl.BlockSpec(memory_space=pltpu.VMEM)] * (len(args) - smem)
    return pl.pallas_call(
        body,
        out_shape=outs,
        in_specs=specs,
        out_specs=[pl.BlockSpec(memory_space=pltpu.VMEM)] * len(outs),
        scratch_shapes=list(scratch),
        compiler_params=pltpu.CompilerParams(vmem_limit_bytes=LIMIT),
    )(*args)


def route_body(ids_ref, map_ref, slot_ref, local_ref, pieces, owners, cells):
    feats, bag, batch = ids_ref.shape
    hi_count, lo_count = map_ref.shape
    mapped = map_ref[...].astype(F32).T
    high = jnp.floor(mapped * (1.0 / 256.0))
    pieces[0:lo_count, :] = (mapped - 256.0 * high).astype(BF)
    pieces[lo_count:, :] = (high - 256.0).astype(BF)
    count = feats * bag
    sums = jnp.zeros((64, 32), F32)
    locs, ys, cs, ms = [], [], [], []
    m_here, y_here = lax.axis_index("mp"), lax.axis_index("replica") >> 1
    lane = iota((1, batch), 1).astype(F32)
    for fl in range(count):
        ids = ids_ref[fl // bag, fl % bag : fl % bag + 1, :]
        hit = onehot(iota((hi_count, batch), 0) == (ids >> 7))
        found = dot(pieces[...], hit)
        mask = iota((lo_count, batch), 0) == (ids & 127)

        def pick(k):
            part = found[k * lo_count : (k + 1) * lo_count, :]
            return jnp.sum(jnp.where(mask, part, 0.0), axis=0, keepdims=True)

        low, high = pick(0).astype(I32), pick(1).astype(I32) + 256
        loc = (low & 127).astype(F32)
        own, y, c = high >> 3, high & 7, low >> 7
        owner = onehot(iota((64, batch), 0) == own ^ m_here)
        cell = jnp.where(iota((16, batch), 0) == c * 8 + (y ^ y_here), 1.0, 0.0)
        owners[fl] = owner
        cells[fl] = cell
        terms = jnp.concatenate([cell * float(fl), cell * lane], axis=0).astype(BF)
        sums += dot_t(owner, terms)
        locs.append(loc)
        ys.append(y)
        cs.append(c)
        ms.append(own)
    total = sums[:, :16] * float(batch) + sums[:, 16:]
    top = jnp.floor(total * (1.0 / 64.0))
    halves = jnp.concatenate([top, total - 64.0 * top], axis=1).T.astype(BF)
    local = jnp.zeros((64, 32), F32)
    for fl in range(count):
        seen = dot(halves, owners[fl])
        pair = jnp.sum(cells[fl] * (64.0 * seen[:16] + seen[16:]), axis=0, keepdims=True)
        rank = (pair < 2.0 * (lane + float(fl * batch))).astype(I32)
        lead = cs[fl] * 2 + rank
        slot_ref[fl : fl + 1, :] = (ys[fl] * 64 + ms[fl]) * 4 + lead
        spread = jnp.where(iota((32, batch), 0) == lead * 8 + (ys[fl] ^ y_here), locs[fl], 0.0)
        local += dot_t(owners[fl], spread.astype(BF))
    turned = local.T
    local_ref[...] = jnp.concatenate([turned[:16], turned[16:]], axis=1)


def pack_body(slot_ref, grads_ref, send_ref):
    batch, wide = grads_ref.shape
    width = 256
    step = 512
    for chunk in range(2048 // step):
        rows = iota((step, batch), 0) + chunk * step
        acc = jnp.zeros((step, width), F32)
        for f in range(wide // width):
            a = slot_ref[2 * f : 2 * f + 1, :]
            b = slot_ref[2 * f + 1 : 2 * f + 2, :]
            take = onehot((rows == a) | (rows == b))
            acc += dot(take, grads_ref[:, f * width : (f + 1) * width])
        left = acc[:, :128].reshape(step // 8, 8, 128)
        right = acc[:, 128:].reshape(step // 8, 8, 128)
        low = iota((step // 8, 8, 128), 1) < 4
        first = jnp.where(low, left, pltpu.roll(right, 4, axis=1))
        second = jnp.where(low, pltpu.roll(left, 4, axis=1), right)
        both = jnp.concatenate([first[:, None], second[:, None]], axis=1)
        send_ref[chunk * 2 * step : (chunk + 1) * 2 * step, :] = both.reshape(2 * step, 128).astype(BF)


def spots_body(local_ref, spots_ref):
    here = lax.axis_index("replica")
    y_here, core = here >> 1, here & 1
    n = iota((128, 512), 1)
    lane = ((n >> 1) & 1) * 64 + ((n >> 3) ^ lax.axis_index("mp"))
    found = dot(local_ref[...].astype(BF), onehot(iota((128, 512), 0) == lane)).astype(BF)
    row = iota((8, 16), 0) ^ y_here
    place = iota((8, 16), 1)
    first = dot(onehot(place == row), found)
    second = dot(onehot(place == row + 8), found)
    n = iota((8, 512), 1)
    spot = jnp.where((n & 1) == 0, first, second).astype(I32)
    spots_ref[...] = spot + ((n >> 2) & 1) * 256 + (((n >> 1) & 1) ^ core) * 128


def total_body(spots_ref, got_ref, own_ref, sib_ref):
    acc = jnp.zeros((512, 128), F32)
    for y in range(8):
        hit = onehot(iota((512, 512), 0) == spots_ref[y : y + 1, :])
        acc += dot(hit, got_ref[y * 512 : (y + 1) * 512, :])
    own_ref[:, :128] = acc[0:128]
    own_ref[:, 128:] = acc[256:384]
    sib_ref[:, :128] = acc[128:256]
    sib_ref[:, 128:] = acc[384:512]


def adam_body(own_ref, sib_ref, moment_ref, second_ref, new_moment_ref, new_second_ref, head_ref, tail_ref):
    grad = own_ref[...] + sib_ref[...]
    moment = BETA_ONE * moment_ref[...] + (1.0 - BETA_ONE) * grad
    mean = jnp.sum(grad * grad, axis=1, keepdims=True) * (1.0 / grad.shape[1])
    rows = grad.shape[0]
    eye = iota((rows, rows), 0) == iota((rows, rows), 1)
    old = jnp.sum(jnp.where(eye, second_ref[...], 0.0), axis=1, keepdims=True)
    second = BETA_TWO * old + (1.0 - BETA_TWO) * mean
    new_moment_ref[...] = moment
    new_second_ref[...] = jnp.sum(jnp.where(eye, second, 0.0), axis=0, keepdims=True)
    step = (LEARN_RATE * moment / (jnp.sqrt(second) + EPSILON)).astype(BF)
    head_ref[...] = step[:HEAD]
    tail_ref[...] = jnp.broadcast_to(step[HEAD:][None], tail_ref.shape)


def table_body(head_ref, tail_ref, table_ref, out_ref, rows_ref, in_sems, out_sems):
    parts = in_sems.shape[0]
    size = rows_ref.shape[0] // parts

    def span(i):
        return pl.ds(i * size, size)

    loads = [
        pltpu.make_async_copy(table_ref.at[span(i)], rows_ref.at[span(i)], in_sems.at[i])
        for i in range(parts)
    ]
    stores = [
        pltpu.make_async_copy(rows_ref.at[span(i)], out_ref.at[span(i)], out_sems.at[i])
        for i in range(parts)
    ]
    for load in loads:
        load.start()
    for i in range(parts):
        loads[i].wait()
        for r in range(i * size // 128, (i + 1) * size // 128):
            mid = r * 128 + HEAD
            rows_ref[r * 128 : mid, :] -= head_ref[r].astype(F32)
            rows_ref[mid : (r + 1) * 128, :] -= tail_ref[r].astype(F32)
        stores[i].start()
    for store in stores:
        store.wait()


def pooled_grads(pooled, labels, w_hidden, b_hidden, w_out):
    batch_rows, num_feats, feat_width = pooled.shape
    features_flat = pooled.reshape(batch_rows, num_feats * feat_width)
    pre_act = jnp.dot(features_flat, w_hidden, preferred_element_type=F32) + b_hidden
    sig_pre = jax.nn.sigmoid(pre_act)
    hidden = pre_act * sig_pre
    logit = jnp.sum(hidden * w_out[None, :], axis=1)
    probability = jax.nn.sigmoid(logit)
    target = labels.astype(F32)
    dlogit = (
        -LOSS_SCALE * (1.0 - probability * probability) * (target - (1.0 - target) * probability)
    )
    dpre = (
        dlogit[:, None] * w_out[None, :] * (sig_pre * (1.0 + pre_act * (1.0 - sig_pre)))
    ).astype(BF)
    dflat = lax.dot_general(
        dpre, w_hidden, (((1,), (1,)), ((), ())), preferred_element_type=F32
    )
    return dflat.astype(BF)


def on_device(
    pooled,
    row_ids,
    labels,
    row_slot,
    w_hidden,
    b_hidden,
    w_out,
    emb_table,
    adam_moment,
    adam_second,
):
    shape = jax.ShapeDtypeStruct
    rep, mp = "replica", "mp"
    same_core = [[2 * y + c for y in range(8)] for c in range(2)]
    planes = [[r * 64 + m for r in group for m in range(64)] for group in same_core]
    other_core = [(i, i ^ 1) for i in range(16)]
    slots, local = call(
        route_body,
        [shape((8, 256), I32), shape((16, 128), F32)],
        row_ids.transpose(1, 2, 0),
        row_slot.reshape(1024, 128),
        scratch=[
            pltpu.VMEM((256, 1024), BF),
            pltpu.VMEM((8, 64, 256), BF),
            pltpu.VMEM((8, 16, 256), F32),
        ],
    )
    rows, lanes = iota((16, 128), 0), iota((16, 128), 1)
    for bit in (1, 2, 4):
        other = lax.ppermute(local, rep, [(i, i ^ (2 * bit)) for i in range(16)])
        local = jnp.where((rows & bit) != 0, other, local)
    grads = pooled_grads(pooled, labels, w_hidden, b_hidden, w_out)
    (send,) = call(pack_body, [shape((4096, 128), BF)], slots, grads)
    send, local = lax.optimization_barrier((send, local))
    got = lax.all_to_all(
        send.reshape(512, 8, 128),
        (rep, mp),
        split_axis=0,
        concat_axis=0,
        tiled=True,
        axis_index_groups=planes,
    )
    for bit in (1, 2, 4, 8, 16, 32):
        other = lax.ppermute(local, mp, [(i, i ^ bit) for i in range(64)])
        local = jnp.where((lanes & bit) != 0, other, local)
    (spots,) = call(spots_body, [shape((8, 512), I32)], local)
    own, sib = call(
        total_body,
        [shape((128, 256), F32), shape((128, 256), F32)],
        spots,
        got.reshape(4096, 128),
    )
    sib = lax.ppermute(sib, rep, other_core)
    new_moment, new_second, head, tail = call(
        adam_body,
        [
            shape((128, 256), F32),
            shape((1, 128), F32),
            shape((HEAD, 256), BF),
            shape((16, 128 - HEAD, 256), BF),
        ],
        own,
        sib,
        adam_moment,
        adam_second.reshape(1, 128),
    )
    tails = lax.all_to_all(tail, rep, split_axis=0, concat_axis=0, tiled=True)
    heads = lax.all_gather(head, rep, axis=0, tiled=False)
    vmem, hbm = pl.BlockSpec(memory_space=pltpu.VMEM), pl.BlockSpec(memory_space=pltpu.HBM)
    new_table = pl.pallas_call(
        table_body,
        out_shape=shape((2048, 256), F32),
        in_specs=[vmem, vmem, hbm],
        out_specs=hbm,
        scratch_shapes=[
            pltpu.VMEM((2048, 256), F32),
            pltpu.SemaphoreType.DMA((4,)),
            pltpu.SemaphoreType.DMA((4,)),
        ],
        compiler_params=pltpu.CompilerParams(vmem_limit_bytes=51 * 1024 * 1024),
    )(heads, tails, emb_table)
    return (new_table, new_moment, new_second.reshape(128))


def solution(mesh):
    in_specs = (
        P(("replica", "mp"), None, None),
        P(("replica", "mp"), None, None),
        P(("replica", "mp")),
        P(),
        P(),
        P(),
        P(),
        P("mp", None),
        P(("mp", "replica"), None),
        P(("mp", "replica")),
    )
    out_specs = (P("mp", None), P(("mp", "replica"), None), P(("mp", "replica")))
    return jax.shard_map(
        on_device, mesh=mesh, in_specs=in_specs, out_specs=out_specs, check_vma=False
    )
```

```python
import jax
import jax.numpy as jnp
from jax import lax
from jax.experimental import pallas as pl
from jax.experimental.pallas import tpu as pltpu
from jax.sharding import PartitionSpec as P

LOSS_SCALE = 128.0
LEARN_RATE = 0.3
BETA_ONE = 0.8
BETA_TWO = 0.99
EPSILON = 1e-08

BF = jnp.bfloat16
F32 = jnp.float32
I32 = jnp.int32
LIMIT = 32 * 1024 * 1024
HEAD = 112


def iota(shape, dim):
    return lax.broadcasted_iota(I32, shape, dim)


def dot(a, b):
    return jnp.dot(a, b, preferred_element_type=F32)


def dot_t(a, b):
    return lax.dot_general(a, b, (((1,), (1,)), ((), ())), preferred_element_type=F32)


def turned_bits(z):
    return ((z & 1) << 3) | ((z & 2) << 1) | ((z & 4) >> 1) | ((z & 8) >> 3)


def onehot(cond):
    return jnp.where(cond, 1.0, 0.0).astype(BF)


def call(body, outs, *args, scratch=(), smem=0, alias=None):
    specs = [pl.BlockSpec(memory_space=pltpu.SMEM)] * smem
    specs += [pl.BlockSpec(memory_space=pltpu.VMEM)] * (len(args) - smem)
    return pl.pallas_call(
        body,
        out_shape=outs,
        in_specs=specs,
        out_specs=[pl.BlockSpec(memory_space=pltpu.VMEM)] * len(outs),
        scratch_shapes=list(scratch),
        compiler_params=pltpu.CompilerParams(vmem_limit_bytes=LIMIT),
    )(*args)


def route_body(ids_ref, map_ref, slot_ref, local_ref, pieces, owners, cells):
    feats, bag, batch = ids_ref.shape
    hi_count, lo_count = map_ref.shape
    mapped = map_ref[...].astype(F32).T
    high = jnp.floor(mapped * (1.0 / 256.0))
    pieces[0:lo_count, :] = (mapped - 256.0 * high).astype(BF)
    pieces[lo_count:, :] = (high - 256.0).astype(BF)
    count = feats * bag
    sums = jnp.zeros((64, 32), F32)
    locs, ys, cs, ms = [], [], [], []
    lane = iota((1, batch), 1).astype(F32)
    for fl in range(count):
        ids = ids_ref[fl // bag, fl % bag : fl % bag + 1, :]
        hit = onehot(iota((hi_count, batch), 0) == (ids >> 7))
        found = dot(pieces[...], hit)
        mask = iota((lo_count, batch), 0) == (ids & 127)

        def pick(k):
            part = found[k * lo_count : (k + 1) * lo_count, :]
            return jnp.sum(jnp.where(mask, part, 0.0), axis=0, keepdims=True)

        low, high = pick(0).astype(I32), pick(1).astype(I32) + 256
        loc = (low & 127).astype(F32)
        own, y, c = high >> 3, high & 7, low >> 7
        owner = onehot(iota((64, batch), 0) == own)
        cell = jnp.where(iota((16, batch), 0) == c * 8 + y, 1.0, 0.0)
        owners[fl] = owner
        cells[fl] = cell
        terms = jnp.concatenate([cell * float(fl), cell * lane], axis=0).astype(BF)
        sums += dot_t(owner, terms)
        locs.append(loc)
        ys.append(y)
        cs.append(c)
        ms.append(own)
    total = sums[:, :16] * float(batch) + sums[:, 16:]
    top = jnp.floor(total * (1.0 / 64.0))
    halves = jnp.concatenate([top, total - 64.0 * top], axis=1).T.astype(BF)
    local = jnp.zeros((64, 32), F32)
    for fl in range(count):
        seen = dot(halves, owners[fl])
        pair = jnp.sum(cells[fl] * (64.0 * seen[:16] + seen[16:]), axis=0, keepdims=True)
        rank = (pair < 2.0 * (lane + float(fl * batch))).astype(I32)
        lead = cs[fl] * 2 + rank
        peer = (ms[fl] & 3) * 128 + ys[fl] * 16 + turned_bits(ms[fl] >> 2)
        slot_ref[fl : fl + 1, :] = peer * 4 + lead
        spread = jnp.where(iota((32, batch), 0) == lead * 8 + ys[fl], locs[fl], 0.0)
        local += dot_t(owners[fl], spread.astype(BF))
    local_ref[...] = local


def pack_body(slot_ref, grads_ref, send_ref):
    batch, wide = grads_ref.shape
    width = 256
    step = 512
    for chunk in range(2048 // step):
        rows = iota((step, batch), 0) + chunk * step
        acc = jnp.zeros((step, width), F32)
        for f in range(wide // width):
            a = slot_ref[2 * f : 2 * f + 1, :]
            b = slot_ref[2 * f + 1 : 2 * f + 2, :]
            take = onehot((rows == a) | (rows == b))
            acc += dot(take, grads_ref[:, f * width : (f + 1) * width])
        left = acc[:, :128].reshape(step // 8, 8, 128)
        right = acc[:, 128:].reshape(step // 8, 8, 128)
        low = iota((step // 8, 8, 128), 1) < 4
        first = jnp.where(low, left, pltpu.roll(right, 4, axis=1))
        second = jnp.where(low, pltpu.roll(left, 4, axis=1), right)
        both = jnp.concatenate([first[:, None], second[:, None]], axis=1)
        send_ref[chunk * 2 * step : (chunk + 1) * 2 * step, :] = both.reshape(2 * step, 128).astype(BF)


def spots_body(place_ref, local_ref, spots_ref):
    y_here, core = place_ref[0], place_ref[1]
    n = iota((32, 512), 1)
    pick = onehot(iota((32, 512), 0) == (n & 3) * 8 + y_here)
    rows = iota((512, 512), 0)
    n = iota((1, 512), 1)
    shift = ((n >> 2) & 1) * 256 + (((n >> 1) & 1) ^ core) * 128
    found = dot(local_ref[...].reshape(512, 32).astype(BF), pick)
    for part in range(8):
        y = (part & 1) * 4 + (n >> 7)
        source = y * 64 + turned_bits((n >> 3) & 15) * 4 + (part >> 1)
        spot = jnp.sum(jnp.where(rows == source, found, 0.0), axis=0, keepdims=True).astype(I32)
        spots_ref[part : part + 1, :] = spot + shift


def total_body(spots_ref, got_ref, own_ref, sib_ref):
    acc = jnp.zeros((512, 128), F32)
    for y in range(8):
        hit = onehot(iota((512, 512), 0) == spots_ref[y : y + 1, :])
        acc += dot(hit, got_ref[y * 512 : (y + 1) * 512, :])
    own_ref[:, :128] = acc[0:128]
    own_ref[:, 128:] = acc[256:384]
    sib_ref[:, :128] = acc[128:256]
    sib_ref[:, 128:] = acc[384:512]


def adam_body(own_ref, sib_ref, moment_ref, second_ref, new_moment_ref, new_second_ref, head_ref, tail_ref):
    grad = own_ref[...] + sib_ref[...]
    moment = BETA_ONE * moment_ref[...] + (1.0 - BETA_ONE) * grad
    mean = jnp.sum(grad * grad, axis=1, keepdims=True) * (1.0 / grad.shape[1])
    rows = grad.shape[0]
    eye = iota((rows, rows), 0) == iota((rows, rows), 1)
    old = jnp.sum(jnp.where(eye, second_ref[...], 0.0), axis=1, keepdims=True)
    second = BETA_TWO * old + (1.0 - BETA_TWO) * mean
    new_moment_ref[...] = moment
    new_second_ref[...] = jnp.sum(jnp.where(eye, second, 0.0), axis=0, keepdims=True)
    step = (LEARN_RATE * moment / (jnp.sqrt(second) + EPSILON)).astype(BF)
    head_ref[...] = step[:HEAD]
    tail_ref[...] = jnp.broadcast_to(step[HEAD:][None], tail_ref.shape)


def table_body(head_ref, tail_ref, table_ref, out_ref, rows_ref, in_sems, out_sems):
    parts = in_sems.shape[0]
    size = rows_ref.shape[0] // parts

    def span(i):
        return pl.ds(i * size, size)

    loads = [
        pltpu.make_async_copy(table_ref.at[span(i)], rows_ref.at[span(i)], in_sems.at[i])
        for i in range(parts)
    ]
    stores = [
        pltpu.make_async_copy(rows_ref.at[span(i)], out_ref.at[span(i)], out_sems.at[i])
        for i in range(parts)
    ]
    for load in loads:
        load.start()
    for i in range(parts):
        loads[i].wait()
        for r in range(i * size // 128, (i + 1) * size // 128):
            mid = r * 128 + HEAD
            rows_ref[r * 128 : mid, :] -= head_ref[r].astype(F32)
            rows_ref[mid : (r + 1) * 128, :] -= tail_ref[r].astype(F32)
        stores[i].start()
    for store in stores:
        store.wait()


def pooled_grads(pooled, labels, w_hidden, b_hidden, w_out):
    batch_rows, num_feats, feat_width = pooled.shape
    features_flat = pooled.reshape(batch_rows, num_feats * feat_width)
    pre_act = jnp.dot(features_flat, w_hidden, preferred_element_type=F32) + b_hidden
    sig_pre = jax.nn.sigmoid(pre_act)
    hidden = pre_act * sig_pre
    logit = jnp.sum(hidden * w_out[None, :], axis=1)
    probability = jax.nn.sigmoid(logit)
    target = labels.astype(F32)
    dlogit = (
        -LOSS_SCALE * (1.0 - probability * probability) * (target - (1.0 - target) * probability)
    )
    dpre = (
        dlogit[:, None] * w_out[None, :] * (sig_pre * (1.0 + pre_act * (1.0 - sig_pre)))
    ).astype(BF)
    dflat = lax.dot_general(
        dpre, w_hidden, (((1,), (1,)), ((), ())), preferred_element_type=F32
    )
    return dflat.astype(BF)


def on_device(
    pooled,
    row_ids,
    labels,
    row_slot,
    w_hidden,
    b_hidden,
    w_out,
    emb_table,
    adam_moment,
    adam_second,
):
    shape = jax.ShapeDtypeStruct
    rep, mp = "replica", "mp"
    same_core = [[2 * y + c for y in range(8)] for c in range(2)]
    planes = [
        [r * 64 + turned_bits(z) * 4 + x for x in range(4) for r in group for z in range(16)]
        for group in same_core
    ]
    other_core = [(i, i ^ 1) for i in range(16)]
    core = lax.axis_index(rep) & 1
    place = jnp.stack([lax.axis_index(rep) >> 1, core]).astype(I32)

    slots, local = call(
        route_body,
        [shape((8, 256), I32), shape((64, 32), F32)],
        row_ids.transpose(1, 2, 0),
        row_slot.reshape(1024, 128),
        scratch=[
            pltpu.VMEM((256, 1024), BF),
            pltpu.VMEM((8, 64, 256), BF),
            pltpu.VMEM((8, 16, 256), F32),
        ],
    )
    local = lax.all_to_all(
        local.reshape(64, 1, 32), mp, split_axis=0, concat_axis=0, tiled=True
    )
    grads = pooled_grads(pooled, labels, w_hidden, b_hidden, w_out)
    (send,) = call(pack_body, [shape((4096, 128), BF)], slots, grads)
    send, local = lax.optimization_barrier((send, local))
    got = lax.all_to_all(
        send.reshape(512, 8, 128),
        (rep, mp),
        split_axis=0,
        concat_axis=0,
        tiled=True,
        axis_index_groups=planes,
    )
    local = lax.all_gather(
        local.reshape(64, 32), rep, axis=0, tiled=False, axis_index_groups=same_core
    )
    (spots,) = call(spots_body, [shape((8, 512), I32)], place, local, smem=1)
    own, sib = call(
        total_body,
        [shape((128, 256), F32), shape((128, 256), F32)],
        spots,
        got.reshape(4096, 128),
    )
    sib = lax.ppermute(sib, rep, other_core)
    new_moment, new_second, head, tail = call(
        adam_body,
        [
            shape((128, 256), F32),
            shape((1, 128), F32),
            shape((HEAD, 256), BF),
            shape((16, 128 - HEAD, 256), BF),
        ],
        own,
        sib,
        adam_moment,
        adam_second.reshape(1, 128),
    )
    tails = lax.all_to_all(tail, rep, split_axis=0, concat_axis=0, tiled=True)
    heads = lax.all_gather(head, rep, axis=0, tiled=False)
    vmem, hbm = pl.BlockSpec(memory_space=pltpu.VMEM), pl.BlockSpec(memory_space=pltpu.HBM)
    new_table = pl.pallas_call(
        table_body,
        out_shape=shape((2048, 256), F32),
        in_specs=[vmem, vmem, hbm],
        out_specs=hbm,
        scratch_shapes=[
            pltpu.VMEM((2048, 256), F32),
            pltpu.SemaphoreType.DMA((4,)),
            pltpu.SemaphoreType.DMA((4,)),
        ],
        compiler_params=pltpu.CompilerParams(vmem_limit_bytes=51 * 1024 * 1024),
    )(heads, tails, emb_table)
    return (new_table, new_moment, new_second.reshape(128))


def solution(mesh):
    in_specs = (
        P(("replica", "mp"), None, None),
        P(("replica", "mp"), None, None),
        P(("replica", "mp")),
        P(),
        P(),
        P(),
        P(),
        P("mp", None),
        P(("mp", "replica"), None),
        P(("mp", "replica")),
    )
    out_specs = (P("mp", None), P(("mp", "replica"), None), P(("mp", "replica")))
    return jax.shard_map(
        on_device, mesh=mesh, in_specs=in_specs, out_specs=out_specs, check_vma=False
    )
```

```python
import jax
import jax.numpy as jnp
from jax import lax
from jax.experimental import pallas as pl
from jax.experimental.pallas import tpu as pltpu
from jax.sharding import PartitionSpec as P

LOSS_SCALE = 128.0
LEARN_RATE = 0.3
BETA_ONE = 0.8
BETA_TWO = 0.99
EPSILON = 1e-08

BF = jnp.bfloat16
F32 = jnp.float32
I32 = jnp.int32
LIMIT = 32 * 1024 * 1024
HEAD = 112


def iota(shape, dim):
    return lax.broadcasted_iota(I32, shape, dim)


def dot(a, b):
    return jnp.dot(a, b, preferred_element_type=F32)


def dot_t(a, b):
    return lax.dot_general(a, b, (((1,), (1,)), ((), ())), preferred_element_type=F32)


def turned_bits(z):
    return ((z & 1) << 3) | ((z & 2) << 1) | ((z & 4) >> 1) | ((z & 8) >> 3)


def onehot(cond):
    return jnp.where(cond, 1.0, 0.0).astype(BF)


def call(body, outs, *args, scratch=(), smem=0, alias=None):
    specs = [pl.BlockSpec(memory_space=pltpu.SMEM)] * smem
    specs += [pl.BlockSpec(memory_space=pltpu.VMEM)] * (len(args) - smem)
    return pl.pallas_call(
        body,
        out_shape=outs,
        in_specs=specs,
        out_specs=[pl.BlockSpec(memory_space=pltpu.VMEM)] * len(outs),
        scratch_shapes=list(scratch),
        compiler_params=pltpu.CompilerParams(vmem_limit_bytes=LIMIT),
    )(*args)


def route_body(ids_ref, map_ref, slot_ref, local_ref, pieces, owners, cells):
    feats, bag, batch = ids_ref.shape
    hi_count, lo_count = map_ref.shape
    mapped = map_ref[...].astype(F32).T
    high = jnp.floor(mapped * (1.0 / 256.0))
    pieces[0:lo_count, :] = (mapped - 256.0 * high).astype(BF)
    pieces[lo_count:, :] = (high - 256.0).astype(BF)
    count = feats * bag
    sums = jnp.zeros((64, 32), F32)
    locs, ys, cs, ms = [], [], [], []
    x_here = lax.axis_index("mp") & 3
    lane = iota((1, batch), 1).astype(F32)
    for fl in range(count):
        ids = ids_ref[fl // bag, fl % bag : fl % bag + 1, :]
        hit = onehot(iota((hi_count, batch), 0) == (ids >> 7))
        found = dot(pieces[...], hit)
        mask = iota((lo_count, batch), 0) == (ids & 127)

        def pick(k):
            part = found[k * lo_count : (k + 1) * lo_count, :]
            return jnp.sum(jnp.where(mask, part, 0.0), axis=0, keepdims=True)

        low, high = pick(0).astype(I32), pick(1).astype(I32) + 256
        loc = (low & 127).astype(F32)
        own, y, c = high >> 3, high & 7, low >> 7
        owner = onehot(iota((64, batch), 0) == ((own & 3) ^ x_here) * 16 + (own >> 2))
        cell = jnp.where(iota((16, batch), 0) == c * 8 + y, 1.0, 0.0)
        owners[fl] = owner
        cells[fl] = cell
        terms = jnp.concatenate([cell * float(fl), cell * lane], axis=0).astype(BF)
        sums += dot_t(owner, terms)
        locs.append(loc)
        ys.append(y)
        cs.append(c)
        ms.append(own)
    total = sums[:, :16] * float(batch) + sums[:, 16:]
    top = jnp.floor(total * (1.0 / 64.0))
    halves = jnp.concatenate([top, total - 64.0 * top], axis=1).T.astype(BF)
    local = jnp.zeros((64, 32), F32)
    for fl in range(count):
        seen = dot(halves, owners[fl])
        pair = jnp.sum(cells[fl] * (64.0 * seen[:16] + seen[16:]), axis=0, keepdims=True)
        rank = (pair < 2.0 * (lane + float(fl * batch))).astype(I32)
        lead = cs[fl] * 2 + rank
        peer = (ms[fl] & 3) * 128 + ys[fl] * 16 + turned_bits(ms[fl] >> 2)
        slot_ref[fl : fl + 1, :] = peer * 4 + lead
        spread = jnp.where(iota((32, batch), 0) == lead * 8 + ys[fl], locs[fl], 0.0)
        local += dot_t(owners[fl], spread.astype(BF))
    parts = [local[16 * x : 16 * (x + 1)] for x in range(4)]
    local_ref[...] = jnp.concatenate(parts, axis=1)


def pack_body(slot_ref, grads_ref, send_ref):
    batch, wide = grads_ref.shape
    width = 256
    step = 512
    for chunk in range(2048 // step):
        rows = iota((step, batch), 0) + chunk * step
        acc = jnp.zeros((step, width), F32)
        for f in range(wide // width):
            a = slot_ref[2 * f : 2 * f + 1, :]
            b = slot_ref[2 * f + 1 : 2 * f + 2, :]
            take = onehot((rows == a) | (rows == b))
            acc += dot(take, grads_ref[:, f * width : (f + 1) * width])
        left = acc[:, :128].reshape(step // 8, 8, 128)
        right = acc[:, 128:].reshape(step // 8, 8, 128)
        low = iota((step // 8, 8, 128), 1) < 4
        first = jnp.where(low, left, pltpu.roll(right, 4, axis=1))
        second = jnp.where(low, pltpu.roll(left, 4, axis=1), right)
        both = jnp.concatenate([first[:, None], second[:, None]], axis=1)
        send_ref[chunk * 2 * step : (chunk + 1) * 2 * step, :] = both.reshape(2 * step, 128).astype(BF)


def spots_body(local_ref, spots_ref):
    here, x_here = lax.axis_index("replica"), lax.axis_index("mp") & 3
    y_here, core = here >> 1, here & 1
    local = local_ref[...].reshape(128, 128).astype(BF)
    lanes, rows = iota((128, 512), 0), iota((128, 512), 0)
    n = iota((1, 512), 1)
    shift = ((n >> 2) & 1) * 256 + (((n >> 1) & 1) ^ core) * 128
    for x in range(4):
        pick = onehot(lanes == (x ^ x_here) * 32 + (n & 3) * 8 + y_here)
        found = dot(local, pick)
        for part in (2 * x, 2 * x + 1):
            y = (part & 1) * 4 + (n >> 7)
            near = rows == y * 16 + turned_bits((n >> 3) & 15)
            spot = jnp.sum(jnp.where(near, found, 0.0), axis=0, keepdims=True).astype(I32)
            spots_ref[part : part + 1, :] = spot + shift


def total_body(spots_ref, got_ref, own_ref, sib_ref):
    acc = jnp.zeros((512, 128), F32)
    for y in range(8):
        hit = onehot(iota((512, 512), 0) == spots_ref[y : y + 1, :])
        acc += dot(hit, got_ref[y * 512 : (y + 1) * 512, :])
    own_ref[:, :128] = acc[0:128]
    own_ref[:, 128:] = acc[256:384]
    sib_ref[:, :128] = acc[128:256]
    sib_ref[:, 128:] = acc[384:512]


def adam_body(own_ref, sib_ref, moment_ref, second_ref, new_moment_ref, new_second_ref, head_ref, tail_ref):
    grad = own_ref[...] + sib_ref[...]
    moment = BETA_ONE * moment_ref[...] + (1.0 - BETA_ONE) * grad
    mean = jnp.sum(grad * grad, axis=1, keepdims=True) * (1.0 / grad.shape[1])
    rows = grad.shape[0]
    eye = iota((rows, rows), 0) == iota((rows, rows), 1)
    old = jnp.sum(jnp.where(eye, second_ref[...], 0.0), axis=1, keepdims=True)
    second = BETA_TWO * old + (1.0 - BETA_TWO) * mean
    new_moment_ref[...] = moment
    new_second_ref[...] = jnp.sum(jnp.where(eye, second, 0.0), axis=0, keepdims=True)
    step = (LEARN_RATE * moment / (jnp.sqrt(second) + EPSILON)).astype(BF)
    head_ref[...] = step[:HEAD]
    tail_ref[...] = jnp.broadcast_to(step[HEAD:][None], tail_ref.shape)


def table_body(head_ref, tail_ref, table_ref, out_ref, rows_ref, in_sems, out_sems):
    parts = in_sems.shape[0]
    size = rows_ref.shape[0] // parts

    def span(i):
        return pl.ds(i * size, size)

    loads = [
        pltpu.make_async_copy(table_ref.at[span(i)], rows_ref.at[span(i)], in_sems.at[i])
        for i in range(parts)
    ]
    stores = [
        pltpu.make_async_copy(rows_ref.at[span(i)], out_ref.at[span(i)], out_sems.at[i])
        for i in range(parts)
    ]
    for load in loads:
        load.start()
    for i in range(parts):
        loads[i].wait()
        for r in range(i * size // 128, (i + 1) * size // 128):
            mid = r * 128 + HEAD
            rows_ref[r * 128 : mid, :] -= head_ref[r].astype(F32)
            rows_ref[mid : (r + 1) * 128, :] -= tail_ref[r].astype(F32)
        stores[i].start()
    for store in stores:
        store.wait()


def pooled_grads(pooled, labels, w_hidden, b_hidden, w_out):
    batch_rows, num_feats, feat_width = pooled.shape
    features_flat = pooled.reshape(batch_rows, num_feats * feat_width)
    pre_act = jnp.dot(features_flat, w_hidden, preferred_element_type=F32) + b_hidden
    sig_pre = jax.nn.sigmoid(pre_act)
    hidden = pre_act * sig_pre
    logit = jnp.sum(hidden * w_out[None, :], axis=1)
    probability = jax.nn.sigmoid(logit)
    target = labels.astype(F32)
    dlogit = (
        -LOSS_SCALE * (1.0 - probability * probability) * (target - (1.0 - target) * probability)
    )
    dpre = (
        dlogit[:, None] * w_out[None, :] * (sig_pre * (1.0 + pre_act * (1.0 - sig_pre)))
    ).astype(BF)
    dflat = lax.dot_general(
        dpre, w_hidden, (((1,), (1,)), ((), ())), preferred_element_type=F32
    )
    return dflat.astype(BF)


def on_device(
    pooled,
    row_ids,
    labels,
    row_slot,
    w_hidden,
    b_hidden,
    w_out,
    emb_table,
    adam_moment,
    adam_second,
):
    shape = jax.ShapeDtypeStruct
    rep, mp = "replica", "mp"
    same_core = [[2 * y + c for y in range(8)] for c in range(2)]
    planes = [
        [r * 64 + turned_bits(z) * 4 + x for x in range(4) for r in group for z in range(16)]
        for group in same_core
    ]
    other_core = [(i, i ^ 1) for i in range(16)]
    slots, local = call(
        route_body,
        [shape((8, 256), I32), shape((16, 128), F32)],
        row_ids.transpose(1, 2, 0),
        row_slot.reshape(1024, 128),
        scratch=[
            pltpu.VMEM((256, 1024), BF),
            pltpu.VMEM((8, 64, 256), BF),
            pltpu.VMEM((8, 16, 256), F32),
        ],
    )
    local = lax.all_to_all(
        local.reshape(16, 1, 128),
        mp,
        split_axis=0,
        concat_axis=0,
        tiled=True,
        axis_index_groups=[[4 * z + x for z in range(16)] for x in range(4)],
    )
    grads = pooled_grads(pooled, labels, w_hidden, b_hidden, w_out)
    (send,) = call(pack_body, [shape((4096, 128), BF)], slots, grads)
    send, local = lax.optimization_barrier((send, local))
    got = lax.all_to_all(
        send.reshape(512, 8, 128),
        (rep, mp),
        split_axis=0,
        concat_axis=0,
        tiled=True,
        axis_index_groups=planes,
    )
    local = local.reshape(16, 128)
    lanes = iota((16, 128), 1)
    for bit in (1, 2):
        other = lax.ppermute(local, mp, [(i, i ^ bit) for i in range(64)])
        local = jnp.where((lanes & (32 * bit)) != 0, other, local)
    local = lax.all_gather(local, rep, axis=0, tiled=False, axis_index_groups=same_core)
    (spots,) = call(spots_body, [shape((8, 512), I32)], local)
    own, sib = call(
        total_body,
        [shape((128, 256), F32), shape((128, 256), F32)],
        spots,
        got.reshape(4096, 128),
    )
    sib = lax.ppermute(sib, rep, other_core)
    new_moment, new_second, head, tail = call(
        adam_body,
        [
            shape((128, 256), F32),
            shape((1, 128), F32),
            shape((HEAD, 256), BF),
            shape((16, 128 - HEAD, 256), BF),
        ],
        own,
        sib,
        adam_moment,
        adam_second.reshape(1, 128),
    )
    tails = lax.all_to_all(tail, rep, split_axis=0, concat_axis=0, tiled=True)
    heads = lax.all_gather(head, rep, axis=0, tiled=False)
    vmem, hbm = pl.BlockSpec(memory_space=pltpu.VMEM), pl.BlockSpec(memory_space=pltpu.HBM)
    new_table = pl.pallas_call(
        table_body,
        out_shape=shape((2048, 256), F32),
        in_specs=[vmem, vmem, hbm],
        out_specs=hbm,
        scratch_shapes=[
            pltpu.VMEM((2048, 256), F32),
            pltpu.SemaphoreType.DMA((4,)),
            pltpu.SemaphoreType.DMA((4,)),
        ],
        compiler_params=pltpu.CompilerParams(vmem_limit_bytes=51 * 1024 * 1024),
    )(heads, tails, emb_table)
    return (new_table, new_moment, new_second.reshape(128))


def solution(mesh):
    in_specs = (
        P(("replica", "mp"), None, None),
        P(("replica", "mp"), None, None),
        P(("replica", "mp")),
        P(),
        P(),
        P(),
        P(),
        P("mp", None),
        P(("mp", "replica"), None),
        P(("mp", "replica")),
    )
    out_specs = (P("mp", None), P(("mp", "replica"), None), P(("mp", "replica")))
    return jax.shard_map(
        on_device, mesh=mesh, in_specs=in_specs, out_specs=out_specs, check_vma=False
    )
```

```python
import jax
import jax.numpy as jnp
from jax import lax
from jax.experimental import pallas as pl
from jax.experimental.pallas import tpu as pltpu
from jax.sharding import PartitionSpec as P

LOSS_SCALE = 128.0
LEARN_RATE = 0.3
BETA_ONE = 0.8
BETA_TWO = 0.99
EPSILON = 1e-08

BF = jnp.bfloat16
F32 = jnp.float32
I32 = jnp.int32
LIMIT = 32 * 1024 * 1024
HEAD = 112


def iota(shape, dim):
    return lax.broadcasted_iota(I32, shape, dim)


def dot(a, b):
    return jnp.dot(a, b, preferred_element_type=F32)


def dot_t(a, b):
    return lax.dot_general(a, b, (((1,), (1,)), ((), ())), preferred_element_type=F32)


def turned_bits(z):
    return ((z & 1) << 3) | ((z & 2) << 1) | ((z & 4) >> 1) | ((z & 8) >> 3)


def onehot(cond):
    return jnp.where(cond, 1.0, 0.0).astype(BF)


def call(body, outs, *args, scratch=(), smem=0, alias=None):
    specs = [pl.BlockSpec(memory_space=pltpu.SMEM)] * smem
    specs += [pl.BlockSpec(memory_space=pltpu.VMEM)] * (len(args) - smem)
    return pl.pallas_call(
        body,
        out_shape=outs,
        in_specs=specs,
        out_specs=[pl.BlockSpec(memory_space=pltpu.VMEM)] * len(outs),
        scratch_shapes=list(scratch),
        compiler_params=pltpu.CompilerParams(vmem_limit_bytes=LIMIT),
    )(*args)


def route_body(ids_ref, map_ref, slot_ref, local_ref, pieces, owners, cells):
    feats, bag, batch = ids_ref.shape
    hi_count, lo_count = map_ref.shape
    mapped = map_ref[...].astype(F32).T
    high = jnp.floor(mapped * (1.0 / 256.0))
    pieces[0:lo_count, :] = (mapped - 256.0 * high).astype(BF)
    pieces[lo_count:, :] = (high - 256.0).astype(BF)
    count = feats * bag
    sums = jnp.zeros((64, 32), F32)
    locs, ys, cs, ms = [], [], [], []
    x_here = lax.axis_index("mp") & 3
    lane = iota((1, batch), 1).astype(F32)
    for fl in range(count):
        ids = ids_ref[fl // bag, fl % bag : fl % bag + 1, :]
        hit = onehot(iota((hi_count, batch), 0) == (ids >> 7))
        found = dot(pieces[...], hit)
        mask = iota((lo_count, batch), 0) == (ids & 127)

        def pick(k):
            part = found[k * lo_count : (k + 1) * lo_count, :]
            return jnp.sum(jnp.where(mask, part, 0.0), axis=0, keepdims=True)

        low, high = pick(0).astype(I32), pick(1).astype(I32) + 256
        loc = (low & 127).astype(F32)
        own, y, c = high >> 3, high & 7, low >> 7
        owner = onehot(iota((64, batch), 0) == ((own & 3) ^ x_here) * 16 + (own >> 2))
        cell = jnp.where(iota((16, batch), 0) == c * 8 + y, 1.0, 0.0)
        owners[fl] = owner
        cells[fl] = cell
        terms = jnp.concatenate([cell * float(fl), cell * lane], axis=0).astype(BF)
        sums += dot_t(owner, terms)
        locs.append(loc)
        ys.append(y)
        cs.append(c)
        ms.append(own)
    total = sums[:, :16] * float(batch) + sums[:, 16:]
    top = jnp.floor(total * (1.0 / 64.0))
    halves = jnp.concatenate([top, total - 64.0 * top], axis=1).T.astype(BF)
    local = jnp.zeros((64, 32), F32)
    for fl in range(count):
        seen = dot(halves, owners[fl])
        pair = jnp.sum(cells[fl] * (64.0 * seen[:16] + seen[16:]), axis=0, keepdims=True)
        rank = (pair < 2.0 * (lane + float(fl * batch))).astype(I32)
        lead = cs[fl] * 2 + rank
        peer = (ms[fl] & 3) * 128 + ys[fl] * 16 + turned_bits(ms[fl] >> 2)
        slot_ref[fl : fl + 1, :] = peer * 4 + lead
        spread = jnp.where(iota((32, batch), 0) == lead * 8 + ys[fl], locs[fl], 0.0)
        local += dot_t(owners[fl], spread.astype(BF))
    parts = [local[16 * x : 16 * (x + 1)] for x in range(4)]
    local_ref[...] = jnp.concatenate(parts, axis=1)


def pack_body(slot_ref, grads_ref, send_ref):
    batch, wide = grads_ref.shape
    width = 256
    step = 512
    for chunk in range(2048 // step):
        rows = iota((step, batch), 0) + chunk * step
        acc = jnp.zeros((step, width), F32)
        for f in range(wide // width):
            a = slot_ref[2 * f : 2 * f + 1, :]
            b = slot_ref[2 * f + 1 : 2 * f + 2, :]
            take = onehot((rows == a) | (rows == b))
            acc += dot(take, grads_ref[:, f * width : (f + 1) * width])
        left = acc[:, :128].reshape(step // 8, 8, 128)
        right = acc[:, 128:].reshape(step // 8, 8, 128)
        low = iota((step // 8, 8, 128), 1) < 4
        first = jnp.where(low, left, pltpu.roll(right, 4, axis=1))
        second = jnp.where(low, pltpu.roll(left, 4, axis=1), right)
        both = jnp.concatenate([first[:, None], second[:, None]], axis=1)
        send_ref[chunk * 2 * step : (chunk + 1) * 2 * step, :] = both.reshape(2 * step, 128).astype(BF)


def spots_body(local_ref, own_ref, sib_ref):
    here, x_here = lax.axis_index("replica"), lax.axis_index("mp") & 3
    y_here, core = here >> 1, here & 1
    local = local_ref[...].reshape(128, 128).astype(BF)
    lanes, rows = iota((128, 512), 0), iota((128, 512), 0)
    n = iota((1, 512), 1)
    shift = ((n >> 2) & 1) * 128
    same = ((n >> 1) & 1) == core
    for x in range(4):
        pick = onehot(lanes == (x ^ x_here) * 32 + (n & 3) * 8 + y_here)
        found = dot(local, pick)
        for part in (2 * x, 2 * x + 1):
            y = (part & 1) * 4 + (n >> 7)
            near = rows == y * 16 + turned_bits((n >> 3) & 15)
            spot = jnp.sum(jnp.where(near, found, 0.0), axis=0, keepdims=True).astype(I32)
            own_ref[part : part + 1, :] = jnp.where(same, spot + shift, -1)
            sib_ref[part : part + 1, :] = jnp.where(same, -1, spot + shift)


def total_body(spots_ref, got_ref, out_ref):
    acc = jnp.zeros((256, 128), F32)
    for part in range(8):
        hit = onehot(iota((256, 512), 0) == spots_ref[part : part + 1, :])
        acc += dot(hit, got_ref[part * 512 : (part + 1) * 512, :])
    out_ref[:, :128] = acc[:128]
    out_ref[:, 128:] = acc[128:]


def adam_body(own_ref, sib_ref, moment_ref, second_ref, new_moment_ref, new_second_ref, head_ref, tail_ref):
    grad = own_ref[...] + sib_ref[...]
    moment = BETA_ONE * moment_ref[...] + (1.0 - BETA_ONE) * grad
    mean = jnp.sum(grad * grad, axis=1, keepdims=True) * (1.0 / grad.shape[1])
    rows = grad.shape[0]
    eye = iota((rows, rows), 0) == iota((rows, rows), 1)
    old = jnp.sum(jnp.where(eye, second_ref[...], 0.0), axis=1, keepdims=True)
    second = BETA_TWO * old + (1.0 - BETA_TWO) * mean
    new_moment_ref[...] = moment
    new_second_ref[...] = jnp.sum(jnp.where(eye, second, 0.0), axis=0, keepdims=True)
    step = (LEARN_RATE * moment / (jnp.sqrt(second) + EPSILON)).astype(BF)
    head_ref[...] = step[:HEAD]
    tail_ref[...] = jnp.broadcast_to(step[HEAD:][None], tail_ref.shape)


def table_body(head_ref, tail_ref, table_ref, out_ref, rows_ref, in_sems, out_sems):
    parts = in_sems.shape[0]
    size = rows_ref.shape[0] // parts

    def span(i):
        return pl.ds(i * size, size)

    loads = [
        pltpu.make_async_copy(table_ref.at[span(i)], rows_ref.at[span(i)], in_sems.at[i])
        for i in range(parts)
    ]
    stores = [
        pltpu.make_async_copy(rows_ref.at[span(i)], out_ref.at[span(i)], out_sems.at[i])
        for i in range(parts)
    ]
    for load in loads:
        load.start()
    for i in range(parts):
        loads[i].wait()
        for r in range(i * size // 128, (i + 1) * size // 128):
            mid = r * 128 + HEAD
            rows_ref[r * 128 : mid, :] -= head_ref[r].astype(F32)
            rows_ref[mid : (r + 1) * 128, :] -= tail_ref[r].astype(F32)
        stores[i].start()
    for store in stores:
        store.wait()


def pooled_grads(pooled, labels, w_hidden, b_hidden, w_out):
    batch_rows, num_feats, feat_width = pooled.shape
    features_flat = pooled.reshape(batch_rows, num_feats * feat_width)
    pre_act = jnp.dot(features_flat, w_hidden, preferred_element_type=F32) + b_hidden
    sig_pre = jax.nn.sigmoid(pre_act)
    hidden = pre_act * sig_pre
    logit = jnp.sum(hidden * w_out[None, :], axis=1)
    probability = jax.nn.sigmoid(logit)
    target = labels.astype(F32)
    dlogit = (
        -LOSS_SCALE * (1.0 - probability * probability) * (target - (1.0 - target) * probability)
    )
    dpre = (
        dlogit[:, None] * w_out[None, :] * (sig_pre * (1.0 + pre_act * (1.0 - sig_pre)))
    ).astype(BF)
    dflat = lax.dot_general(
        dpre, w_hidden, (((1,), (1,)), ((), ())), preferred_element_type=F32
    )
    return dflat.astype(BF)


def on_device(
    pooled,
    row_ids,
    labels,
    row_slot,
    w_hidden,
    b_hidden,
    w_out,
    emb_table,
    adam_moment,
    adam_second,
):
    shape = jax.ShapeDtypeStruct
    rep, mp = "replica", "mp"
    same_core = [[2 * y + c for y in range(8)] for c in range(2)]
    planes = [
        [r * 64 + turned_bits(z) * 4 + x for x in range(4) for r in group for z in range(16)]
        for group in same_core
    ]
    other_core = [(i, i ^ 1) for i in range(16)]
    slots, local = call(
        route_body,
        [shape((8, 256), I32), shape((16, 128), F32)],
        row_ids.transpose(1, 2, 0),
        row_slot.reshape(1024, 128),
        scratch=[
            pltpu.VMEM((256, 1024), BF),
            pltpu.VMEM((8, 64, 256), BF),
            pltpu.VMEM((8, 16, 256), F32),
        ],
    )
    local = lax.all_to_all(
        local.reshape(16, 1, 128),
        mp,
        split_axis=0,
        concat_axis=0,
        tiled=True,
        axis_index_groups=[[4 * z + x for z in range(16)] for x in range(4)],
    )
    grads = pooled_grads(pooled, labels, w_hidden, b_hidden, w_out)
    (send,) = call(pack_body, [shape((4096, 128), BF)], slots, grads)
    send, local = lax.optimization_barrier((send, local))
    got = lax.all_to_all(
        send.reshape(512, 8, 128),
        (rep, mp),
        split_axis=0,
        concat_axis=0,
        tiled=True,
        axis_index_groups=planes,
    )
    local = local.reshape(16, 128)
    lanes = iota((16, 128), 1)
    for bit in (1, 2):
        other = lax.ppermute(local, mp, [(i, i ^ bit) for i in range(64)])
        local = jnp.where((lanes & (32 * bit)) != 0, other, local)
    local = lax.all_gather(local, rep, axis=0, tiled=False, axis_index_groups=same_core)
    spots = call(spots_body, [shape((8, 512), I32)] * 2, local)
    got = got.reshape(4096, 128)
    (sib,) = call(total_body, [shape((128, 256), F32)], spots[1], got)
    (own,) = call(total_body, [shape((128, 256), F32)], spots[0], got)
    sib = lax.ppermute(sib, rep, other_core)
    new_moment, new_second, head, tail = call(
        adam_body,
        [
            shape((128, 256), F32),
            shape((1, 128), F32),
            shape((HEAD, 256), BF),
            shape((16, 128 - HEAD, 256), BF),
        ],
        own,
        sib,
        adam_moment,
        adam_second.reshape(1, 128),
    )
    tails = lax.all_to_all(tail, rep, split_axis=0, concat_axis=0, tiled=True)
    heads = lax.all_gather(head, rep, axis=0, tiled=False)
    vmem, hbm = pl.BlockSpec(memory_space=pltpu.VMEM), pl.BlockSpec(memory_space=pltpu.HBM)
    new_table = pl.pallas_call(
        table_body,
        out_shape=shape((2048, 256), F32),
        in_specs=[vmem, vmem, hbm],
        out_specs=hbm,
        scratch_shapes=[
            pltpu.VMEM((2048, 256), F32),
            pltpu.SemaphoreType.DMA((4,)),
            pltpu.SemaphoreType.DMA((4,)),
        ],
        compiler_params=pltpu.CompilerParams(vmem_limit_bytes=51 * 1024 * 1024),
    )(heads, tails, emb_table)
    return (new_table, new_moment, new_second.reshape(128))


def solution(mesh):
    in_specs = (
        P(("replica", "mp"), None, None),
        P(("replica", "mp"), None, None),
        P(("replica", "mp")),
        P(),
        P(),
        P(),
        P(),
        P("mp", None),
        P(("mp", "replica"), None),
        P(("mp", "replica")),
    )
    out_specs = (P("mp", None), P(("mp", "replica"), None), P(("mp", "replica")))
    return jax.shard_map(
        on_device, mesh=mesh, in_specs=in_specs, out_specs=out_specs, check_vma=False
    )
```
